32 devices in a mesh: tm: 4 (over z), row: 2 (over x), obs: 4 (over y, core).
Axes of the slice: x: 2, y: 2, z: 4, core: 2. Of those that a mesh axis runs over, the one named last changes fastest.
Arguments:
- dyn_pattern: int32 [8, 8, 3], P('tm'), may hold values from 0 to 7
- dyn_values: float32 [8, 1024, 384], P('tm', ('row', 'obs')), may hold values from -0.3125 to 0.3125
- offsets: float32 [8, 1024], P('tm', ('row', 'obs')), may hold values from -6 to 6
- covariance: float32 [8, 1024, 1024], P('tm', ('row', 'obs')), may hold values from -1 to 14, as said below
- obs_block: int32 [8, 128], P('tm'), may hold values from 0 to 7
- obs_matrix: float32 [8, 128, 256], P('tm', 'obs'), may hold values from -0.375 to 0.375
- obs_data: float32 [8, 128], P('tm', 'obs'), may hold values from -6 to 6
Outputs:
- scan_dynamics: float32 [4, 1024, 1024], P('tm', ('row', 'obs'))
- scan_offset: float32 [4, 1024], P('tm', ('row', 'obs'))
- scan_covariance: float32 [4, 1024, 1024], P('tm', ('row', 'obs'))
- scan_factor: float32 [4, 1024, 512], P('tm', ('row', 'obs'))
- scan_information: float32 [4, 1024], P('tm', ('row', 'obs'))
The draws below stay inside these ranges and needn't reach their ends.
Inputs may be any that keep to these rules, and one draw needn't show every extreme that they name: `dyn_pattern`: each entry names a block column. `obs_block`: each entry names a state block. Each covariance is symmetric and positive definite.
All inputs are finite; a program needn't handle non-finite values.
Results may differ from the reference program's by a relative error of at most 0.00019.
Values sent between devices are 32-bit elements; how exact they have to be, the bound alone decides.
No kernel may reach another device: no remote copies, remote signals or barrier semaphores. Data moves between devices by JAX's collectives and lax.ppermute only.
A program may use at most 128 MiB of HBM per device.

```python
import math
import jax
import jax.numpy as jnp
from jax import lax

STATES = 1024
BLK = 128
KBLK = 3
NBLK = 8
OBS = 128
ELEMS = 8
N_TM = 4


def draw_covariance(key, part):
    keys = jax.random.split(jax.random.fold_in(key, 17), 2)
    spread_scale = 1.5 / math.sqrt(STATES)
    raw = jax.random.uniform(keys[0], (ELEMS, STATES, STATES), jnp.float32, -1.0, 1.0) * spread_scale
    symmetric = 0.5 * (raw + jnp.swapaxes(raw, 1, 2))
    diagonal = jax.random.uniform(keys[1], (ELEMS, STATES), jnp.float32, 2.0, 3.5)
    positions = jnp.arange(STATES)
    on_diagonal = positions[:, None] == positions[None, :]
    matrix = jnp.where(on_diagonal[None, :, :], diagonal[:, :, None], symmetric)
    return matrix


def touch_ends(array, rng, least, largest):
    index_at = [jax.random.randint(jax.random.fold_in(rng, axis), (), 0, length) for axis, length in enumerate(array.shape)]
    widest = array.shape.index(max(array.shape))
    beside = index_at[:widest] + [(index_at[widest] + 1) % array.shape[widest]] + index_at[widest + 1:]
    return array.at[tuple(index_at)].set(least).at[tuple(beside)].set(largest)


def block_levels(own_key, dims, shards, least, top_value):
    def one(dim, shards_of):
        draws = jax.random.uniform(jax.random.fold_in(jax.random.fold_in(own_key, 6), dim), (shards_of,), jnp.float32, least / len(shards), top_value / len(shards))
        return jnp.repeat(jnp.exp(draws), dims[dim] // shards_of).reshape((-1,) + (1,) * (len(dims) - dim - 1))

    gain = one(*shards[0])
    for cut in shards[1:]:
        gain = gain * one(*cut)
    return gain


def scatter_about(rng, extent, width, most, shards=(), kind=jnp.bfloat16):
    level = block_levels(rng, extent, shards, -0.22, 0.18) if shards else 1.0
    array = jax.random.normal(rng, extent, jnp.float32) * width * level
    return jnp.minimum(jnp.maximum(array, -most), most).astype(kind)


def setup_inputs(seed: int = 0) -> dict:
    splits = jax.random.split(jax.random.key(seed), 8)
    return {
        "dyn_pattern": touch_ends(jax.random.randint(splits[0], (ELEMS, NBLK, KBLK), 0, NBLK), jax.random.fold_in(splits[0], 1), 0, NBLK - 1).astype(jnp.int32),
        "dyn_values": scatter_about(splits[1], (ELEMS, STATES, KBLK * BLK), (KBLK * BLK) ** -0.5, 0.3125, ((0, 4), (1, 8)), jnp.float32),
        "offsets": scatter_about(splits[2], (ELEMS, STATES), 1.0, 6.0, ((0, 4), (1, 8)), jnp.float32),
        "covariance": draw_covariance(jax.random.fold_in(splits[7], 71), 0),
        "obs_block": touch_ends(jax.random.randint(splits[4], (ELEMS, OBS), 0, NBLK), jax.random.fold_in(splits[4], 1), 0, NBLK - 1).astype(jnp.int32),
        "obs_matrix": scatter_about(splits[5], (ELEMS, OBS, 2 * BLK), (2 * BLK) ** -0.5, 0.375, ((0, 4), (1, 4)), jnp.float32),
        "obs_data": scatter_about(splits[6], (ELEMS, OBS), 1.0, 6.0, ((0, 4), (1, 4)), jnp.float32),
    }


largest_value = lax.Precision.HIGHEST

def product(left, right):
    return jnp.dot(left.astype(jnp.float32), right.astype(jnp.float32), precision=largest_value, preferred_element_type=jnp.float32)

def lower_solve(lower, rhs):
    return lax.linalg.triangular_solve(lower, rhs, left_side=True, lower=True)

def assemble_dynamics(pattern, values):
    number_of_blocks = pattern.shape[0]
    per_row = pattern.shape[1]
    states = values.shape[0]
    block_extent = states // number_of_blocks
    indicator_matrix = (pattern[:, :, None] == jnp.arange(number_of_blocks, dtype=jnp.int32)[None, None, :]).astype(jnp.float32)
    blocks = values.reshape(number_of_blocks, block_extent, per_row, block_extent)
    return jnp.einsum('ckd,cikj->cidj', indicator_matrix, blocks, precision=largest_value).reshape(states, states)

def assemble_factor(indices, matrix, number_of_blocks):
    item_count = matrix.shape[0]
    block_extent = matrix.shape[1] // 2
    reach = (indices[:, None] + jnp.arange(2, dtype=jnp.int32)[None, :]) % number_of_blocks
    indicator_matrix = (reach[:, :, None] == jnp.arange(number_of_blocks, dtype=jnp.int32)[None, None, :]).astype(jnp.float32)
    piece_list = matrix.reshape(item_count, 2, block_extent)
    return jnp.einsum('onr,onz->rzo', indicator_matrix, piece_list, precision=largest_value).reshape(number_of_blocks * block_extent, item_count)

def combine(prior_dyn, prior_offsets, prior_cov, prior_factor, prior_zeta, own_dyn, own_offsets, own_cov, own_factor, own_zeta):
    rank_width = own_factor.shape[1]
    gain_rows = product(prior_cov, own_factor)
    system = jnp.eye(rank_width, dtype=jnp.float32) + product(own_factor.T, gain_rows)
    lower = jnp.linalg.cholesky(system)
    carried = product(own_dyn, gain_rows)
    observed = product(prior_dyn.T, own_factor)
    upper_part = lower_solve(lower, observed.T)
    weights = lower_solve(lower, carried.T).T
    new_dyn = product(own_dyn, prior_dyn) - product(weights, upper_part)
    new_cov = product(own_dyn, product(prior_cov, own_dyn.T)) - product(weights, weights.T) + own_cov
    residual = own_zeta - product(own_factor.T, prior_offsets)
    solved = lower_solve(lower, residual[:, None])[:, 0]
    new_offsets = product(own_dyn, prior_offsets) + product(weights, solved) + own_offsets
    new_factor = jnp.concatenate([upper_part.T, prior_factor], axis=1)
    new_zeta = jnp.concatenate([solved, prior_zeta])
    return (new_dyn, new_offsets, new_cov, new_factor, new_zeta)

def reference(dyn_pattern, dyn_values, offsets, covariance, obs_block, obs_matrix, obs_data):
    level_one = []
    for pair_index in range(N_TM):
        elements = []
        for slot_index in range(2):
            element_index = 2 * pair_index + slot_index
            dynamics = assemble_dynamics(dyn_pattern[element_index], dyn_values[element_index])
            factor = assemble_factor(obs_block[element_index], obs_matrix[element_index], NBLK)
            elements.append((dynamics, offsets[element_index], covariance[element_index], factor, obs_data[element_index]))
        level_one.append(combine(*elements[0], *elements[1]))
    level_two = []
    for quad_index in range(N_TM // 2):
        level_two.append(combine(*level_one[2 * quad_index], *level_one[2 * quad_index + 1]))
    dyn_list, off_list, cov_list, fac_list, info_list = ([], [], [], [], [])
    for turn_index in range(N_TM):
        if turn_index % 2 == 0:
            dynamics, offset_vec, cov_mat, factor, zeta_vec = level_two[turn_index // 2]
        else:
            dynamics, offset_vec, cov_mat, factor, zeta_vec = level_one[turn_index]
            factor = jnp.concatenate([factor, jnp.zeros((STATES, 2 * OBS), jnp.float32)], axis=1)
            zeta_vec = jnp.concatenate([zeta_vec, jnp.zeros((2 * OBS,), jnp.float32)])
        dyn_list.append(dynamics)
        off_list.append(offset_vec)
        cov_list.append(cov_mat)
        fac_list.append(factor)
        info_list.append(product(factor, zeta_vec))
    return (jnp.stack(dyn_list), jnp.stack(off_list), jnp.stack(cov_list), jnp.stack(fac_list), jnp.stack(info_list))
```

```python
import jax
import jax.numpy as jnp
from jax import lax
from jax.experimental import pallas as pl
from jax.experimental.pallas import tpu as pltpu
from jax.sharding import PartitionSpec as P

F32 = jnp.float32
BF16 = jnp.bfloat16
NN = (((1,), (0,)), ((), ()))
NT = (((1,), (1,)), ((), ()))
PLANE = ("row", "obs")
SMALL = 8


def split(x):
    high = x.astype(BF16)
    return high, (x - high.astype(F32)).astype(BF16)


def dot3(left, right, dims):
    def one(a, b):
        return lax.dot_general(a, b, dims, preferred_element_type=F32)

    return one(left[0], right[0]) + (one(left[0], right[1]) + one(left[1], right[0]))


def mm(left, right, dims=NN):
    return dot3(split(left), split(right), dims)


def reciprocal(x):
    y = pl.reciprocal(x, approx=True)
    return y * (2.0 - x * y)


def inverse_root(x):
    y = lax.rsqrt(x)
    return y * (1.5 - (0.5 * x) * (y * y))


def inverse_factor(matrix):
    size = matrix.shape[0]
    tiles = size // 8
    sub = lax.broadcasted_iota(jnp.int32, (8, size), 0)
    lane = lax.broadcasted_iota(jnp.int32, (8, size), 1)

    def wide(x):
        return jnp.broadcast_to(x, (8, size))

    rows = [matrix[8 * t : 8 * t + 8, :] for t in range(tiles)]
    inverse = [jnp.where(lane == sub + 8 * t, 1.0, 0.0).astype(F32) for t in range(tiles)]
    for p in range(tiles):
        column = {
            (t, c): wide(rows[t][:, 8 * p + c : 8 * p + c + 1])
            for t in range(p, tiles)
            for c in range(8)
        }
        scale = None
        for r in range(8):
            pivot = wide(column[p, r][r : r + 1, :])
            over = reciprocal(pivot)
            root = inverse_root(pivot)
            scale = root if r == 0 else jnp.where(sub == r, root, scale)
            factor = {t: column[t, r] * over for t in range(p, tiles)}
            for c in range(r + 1, 8):
                other = wide(column[p, r][c : c + 1, :])
                for t in range(p, tiles):
                    column[t, c] = column[t, c] - factor[t] * other
            factor[p] = jnp.where(sub > r, factor[p], 0.0)
            row_here = wide(rows[p][r : r + 1, :])
            inverse_here = wide(inverse[p][r : r + 1, :])
            for t in range(p, tiles):
                rows[t] = rows[t] - factor[t] * row_here
                inverse[t] = inverse[t] - factor[t] * inverse_here
        inverse[p] = inverse[p] * scale
    return jnp.concatenate(inverse, axis=0)


def identity(size):
    sub = lax.broadcasted_iota(jnp.int32, (size, size), 0)
    lane = lax.broadcasted_iota(jnp.int32, (size, size), 1)
    return jnp.where(sub == lane, 1.0, 0.0).astype(F32)


def dense_factor(matrix, blocks, number):
    items, width = matrix.shape[0], matrix.shape[1] // 2
    at = jnp.transpose(jnp.broadcast_to(blocks.astype(F32), (width, items)))
    pieces = []
    for r in range(number):
        first = jnp.where(at == float(r), matrix[:, :width], 0.0)
        second = jnp.where(at == float((r - 1) % number), matrix[:, width:], 0.0)
        pieces.append(first + second)
    return jnp.concatenate(pieces, axis=1)


def call(body, name, out_shapes, args, specs, scratch=(), flops=0, out_specs=None):
    whole = pl.BlockSpec(memory_space=pltpu.VMEM)
    return pl.pallas_call(
        body,
        name=name,
        grid=(1,),
        in_specs=specs,
        out_specs=out_specs or [whole] * len(out_shapes),
        out_shape=[jax.ShapeDtypeStruct(s, F32) for s in out_shapes],
        scratch_shapes=list(scratch),
        compiler_params=pltpu.CompilerParams(vmem_limit_bytes=56 * 2**20),
        cost_estimate=pl.CostEstimate(flops=flops, bytes_accessed=2**20, transcendentals=0),
    )(*args)


VM = pl.BlockSpec(memory_space=pltpu.VMEM)
SM = pl.BlockSpec(memory_space=pltpu.SMEM)


def element(shape, which):
    return pl.BlockSpec((1,) + tuple(shape[1:]), lambda i: (which,) + (0,) * (len(shape) - 1))


class Plan:
    def __init__(self, mesh, pattern, values, obs_block, obs_matrix):
        self.row, self.obs = mesh.shape["row"], mesh.shape["obs"]
        self.tm = mesh.shape["tm"]
        self.n = self.row * self.obs
        self.number, self.per_row = pattern.shape[1:]
        self.panel = values.shape[1]
        self.states = self.panel * self.n
        self.width = self.states // self.number
        self.items = obs_block.shape[1]
        self.share = obs_matrix.shape[1]
        self.swapped = self.n == 8 and self.panel % 128 == 0

    def source(self, info, k):
        return lax.bitwise_xor(info[0], k) if self.swapped else k

    def rows_of(self, info, k):
        start = self.source(info, k) * self.panel
        return pl.ds(pl.multiple_of(start, self.panel) if self.swapped else start, self.panel)


def exchange(x, axes, mask, size):
    return lax.ppermute(x, axes, [(a, a ^ mask) for a in range(size)])


def gather(plan, x):
    if plan.swapped:
        even = jnp.stack([x] + [exchange(x, PLANE, k, plan.n) for k in (2, 4, 6)])
        return even, exchange(even, PLANE, 1, plan.n)
    everything = lax.all_gather(x, PLANE, axis=0)
    return everything[0::2], everything[1::2]


def swap_blocks(plan, x):
    return lax.all_to_all(x, PLANE, 0, 0, tiled=True)


def earlier(plan, x):
    return lax.ppermute(x, "tm", [(i, i - 1) for i in range(1, plan.tm)])


def gain_step(plan, info, ints, pieces, covariance, offsets, data):
    share, panel, items = plan.share, plan.panel, plan.items

    def body(info, ints, *refs):
        parts = refs[: plan.obs]
        cov, off, dat, message, obs = refs[plan.obs :]
        for k, part in enumerate(parts):
            start = pl.multiple_of(lax.bitwise_xor(info[1], k) * share, share)
            obs[:, pl.ds(start, share), :] = part[...]
        factor = dense_factor(obs[1], ints[1:2, :items], plan.number)
        message[:panel, :] = mm(cov[0], factor, NT)
        message[panel:, :] = jnp.zeros((SMALL, items), F32)
        message[panel : panel + 2, :panel] = off[...]
        spread = jnp.concatenate([dat[...], jnp.zeros((2, items - share), F32)], axis=1)
        spread = jnp.concatenate([spread, jnp.zeros((6, items), F32)], axis=0)
        message[panel + 2 : panel + 4, :] = pltpu.roll(spread, info[1] * share, 1)[:2]

    return call(
        body,
        "gain",
        [(panel + SMALL, items), (2, items, 2 * plan.width)],
        (info, ints, *pieces, covariance, offsets, data),
        [SM, VM] + [VM] * plan.obs + [element(covariance.shape, 0), VM, VM],
        flops=2**27,
    )


def system_step(plan, info, ints, even, odd, obs):
    states, items, panel = plan.states, plan.items, plan.panel

    def body(info, ints, even, odd, obs, pack):
        tail = states + items
        zeta = jnp.zeros((2, items), F32)
        pack[tail:, :] = jnp.zeros((SMALL * plan.number, items), F32)
        for k in range(plan.n):
            piece = (even, odd)[k % 2]
            pack[plan.rows_of(info, k), :] = piece[k // 2, :panel, :]
            start = plan.source(info, k) * panel
            if plan.swapped:
                block = start // plan.width
                at = pl.multiple_of(tail + block * SMALL, SMALL)
                pack[pl.ds(at, 2), :] = piece[k // 2, panel : panel + 2, :]
            else:
                at = tail + start // plan.width * SMALL
                lane = start % plan.width
                pack[at : at + 2, lane : lane + panel] = piece[k // 2, panel : panel + 2, :panel]
            if k < plan.obs:
                zeta = zeta + piece[k // 2, panel + 2 : panel + 4, :]
        pack[tail + 2 : tail + 4, :] = zeta
        factor = dense_factor(obs[0], ints[1:2, :items], plan.number)
        system = identity(items) + mm(factor, pack[:states, :])
        pack[states:tail, :] = inverse_factor(system)

    return call(
        body,
        "system",
        [(states + items + SMALL * plan.number, items)],
        (info, ints, even, odd, obs),
        [SM, VM, VM, VM, element(obs.shape, 1)],
        flops=2**30,
    )[0]


def spread_step(plan, info, ints, even, odd, covariance):
    states, panel, width = plan.states, plan.panel, plan.width
    wide = plan.per_row * width

    def body(info, ints, even, odd, cov, out, values):
        for k in range(plan.n):
            values[:, plan.rows_of(info, k), :] = (even, odd)[k % 2][k // 2]
        for c in range(plan.number):
            taken = [
                cov[0, :, pl.ds(pl.multiple_of(ints[1, plan.items + c * plan.per_row + k] * width, width), width)]
                for k in range(plan.per_row)
            ]
            out[c * width : (c + 1) * width, :] = mm(
                values[1, c * width : (c + 1) * width, :], jnp.concatenate(taken, axis=1), NT
            )

    return call(
        body,
        "spread",
        [(states, panel), (2, states, wide)],
        (info, ints, even, odd, covariance),
        [SM, SM, VM, VM, element(covariance.shape, 0)],
        flops=2**28,
    )


def assemble_step(plan, info, even, odd):
    states = plan.states
    wide = plan.per_row * plan.width

    def body(info, even, odd, values):
        for k in range(plan.n):
            values[:, plan.rows_of(info, k), :] = (even, odd)[k % 2][k // 2]

    return call(body, "assemble", [(2, states, wide)], (info, even, odd), [SM, VM, VM])[0]


def level_step(plan, ints, values, pack, obs):
    states, items, width, number, per_row = (
        plan.states,
        plan.items,
        plan.width,
        plan.number,
        plan.per_row,
    )
    tail = states + items

    def body(ints, ints_v, values, pack, obs, dyn, weights, upper, small, dense, high, low, up_h, up_l):
        def block(e, c, k):
            return pl.multiple_of(ints[e, items + c * per_row + k] * width, width)

        def rows(c):
            return pl.ds(pl.multiple_of(c * width, width), width)

        def build(c, carry):
            dense[...] = jnp.zeros_like(dense)
            for k in range(per_row):
                at = pl.ds(block(0, c, k), width)
                dense[:, at] = dense[:, at] + values[0, rows(c), k * width : (k + 1) * width]
            high[rows(c), :], low[rows(c), :] = split(dense[...])
            return carry

        lax.fori_loop(0, number, build, 0)
        inverse = pack[states:tail, :]
        factor = dense_factor(obs[1], ints_v[1:2, :items], number)
        factor_pair = split(factor)
        inverse_pair = split(inverse)
        tile = min(256, states)

        def raise_tile(j, carry):
            at = pl.ds(pl.multiple_of(j * tile, tile), tile)
            seen = dot3(factor_pair, (high[:, at], low[:, at]), NN)
            part = dot3(inverse_pair, split(seen), NN)
            upper[:, at] = part
            up_h[:, at], up_l[:, at] = split(part)
            return carry

        lax.fori_loop(0, states // tile, raise_tile, 0)
        vector = jnp.concatenate(
            [pack[tail + c * SMALL : tail + (c + 1) * SMALL, :] for c in range(number)], axis=1
        )
        zeta = pack[tail : tail + SMALL, :]
        residual = zeta[3:4, :] - mm(vector, factor, NT)[0:1, :]
        solved = mm(jnp.broadcast_to(residual, (SMALL, items)), inverse, NT)
        solved_pair = split(solved)
        small[...] = jnp.zeros_like(small)
        small[1:2, :items] = solved[0:1, :]
        small[2:3, :items] = zeta[2:3, :]

        def combine(c, carry):
            own = values[1, rows(c), :]
            own_pair = split(own)
            starts = [block(1, c, k) for k in range(per_row)]
            gains = jnp.concatenate([pack[pl.ds(s, width), :] for s in starts], axis=0)
            carried = dot3(own_pair, split(gains), NN)
            weight = dot3(split(carried), inverse_pair, NT)
            weights[rows(c), :] = weight
            weight_pair = split(weight)
            left = tuple(jnp.concatenate([a, -b], axis=1) for a, b in zip(own_pair, weight_pair))
            right = tuple(
                jnp.concatenate([a[pl.ds(s, width), :] for s in starts] + [b[...]], axis=0)
                for a, b in ((high, up_h), (low, up_l))
            )
            dyn[rows(c), :] = dot3(left, right, NN)
            taken = jnp.concatenate(
                [
                    pack[pl.ds(pl.multiple_of(tail + ints[1, items + c * per_row + k] * SMALL, SMALL), SMALL), :]
                    for k in range(per_row)
                ],
                axis=1,
            )
            moved = dot3(split(taken), own_pair, NT) + dot3(solved_pair, weight_pair, NT)
            own_offset = pack[pl.ds(pl.multiple_of(tail + c * SMALL, SMALL), SMALL), :]
            small[0:1, pl.ds(pl.multiple_of(c * width, width), width)] = moved[0:1, :] + own_offset[1:2, :]
            return carry

        lax.fori_loop(0, number, combine, 0)

    return call(
        body,
        "level",
        [(states, states), (states, items), (items, states), (SMALL, states)],
        (ints, ints, values, pack, obs),
        [SM, VM, VM, VM, VM],
        scratch=[
            pltpu.VMEM((width, states), F32),
            pltpu.VMEM((states, states), BF16),
            pltpu.VMEM((states, states), BF16),
            pltpu.VMEM((items, states), BF16),
            pltpu.VMEM((items, states), BF16),
        ],
        flops=2**32,
    )


def covariance_step(plan, info, ints, moved, values, weights, covariance):
    states, panel, width, items = plan.states, plan.panel, plan.width, plan.items

    def body(info, ints, moved, values, weights, cov, out, held):
        for a in range(plan.n):
            held[:, a * panel : (a + 1) * panel] = moved[a]
        own = weights[pl.ds(pl.multiple_of(info[0] * panel, panel), panel), :]
        for c in range(plan.number):
            taken = [
                held[:, pl.ds(pl.multiple_of(ints[1, items + c * plan.per_row + k] * width, width), width)]
                for k in range(plan.per_row)
            ]
            at = slice(c * width, (c + 1) * width)
            left = jnp.concatenate(taken + [-own], axis=1)
            right = jnp.concatenate([values[0, at, :], weights[at, :]], axis=1)
            out[:, at] = mm(left, right, NT) + cov[0, :, at]

    return call(
        body,
        "covariance",
        [(panel, states)],
        (info, ints, moved, values, weights, covariance),
        [SM, SM, VM, element(values.shape, 1), VM, element(covariance.shape, 1)],
        scratch=[pltpu.VMEM((panel, states), F32)],
        flops=2**28,
    )[0]


def later_gain_step(plan, ints, cov, upper, obs):
    items = plan.items

    def body(ints, cov, upper, obs, out):
        factor = jnp.concatenate([upper[...], dense_factor(obs[0], ints[0:1, :items], plan.number)], axis=0)
        out[...] = mm(cov[...], factor, NT)

    return call(
        body,
        "later_gain",
        [(plan.panel, 2 * items)],
        (ints, cov, upper, obs),
        [VM, VM, VM, element(obs.shape, 0)],
        flops=2**28,
    )[0]


def later_spread_step(plan, dyn, cov):
    def body(dyn, cov, out):
        pair = split(cov[...])
        tile = plan.width

        def one(c, carry):
            at = pl.ds(pl.multiple_of(c * tile, tile), tile)
            out[at, :] = dot3(split(dyn[at, :]), pair, NT)
            return carry

        lax.fori_loop(0, plan.states // tile, one, 0)

    return call(
        body, "later_spread", [(plan.states, plan.panel)], (dyn, cov), [VM, VM], flops=2**29
    )[0]


def later_system_step(plan, info, ints, even, odd, upper, obs):
    states, items, panel = plan.states, plan.items, plan.panel

    def body(info, ints, even, odd, upper, obs, gains, inverse):
        for k in range(plan.n):
            gains[plan.rows_of(info, k), :] = (even, odd)[k % 2][k // 2]
        pair = split(gains[...])
        first = dot3(split(upper[...]), pair, NN)
        other = dense_factor(obs[0], ints[0:1, :items], plan.number)
        second = dot3(split(other), pair, NN)
        top = inverse_factor(identity(items) + first[:, :items])
        lower = mm(second[:, :items], top, NT)
        rest = identity(items) + second[:, items:] - mm(lower, lower, NT)
        bottom = inverse_factor(rest)
        inverse[:items, :items] = top
        inverse[:items, items:] = jnp.zeros((items, items), F32)
        inverse[items:, :items] = -mm(bottom, mm(lower, top))
        inverse[items:, items:] = bottom

    return call(
        body,
        "later_system",
        [(states, 2 * items), (2 * items, 2 * items)],
        (info, ints, even, odd, upper, obs),
        [SM, VM, VM, VM, VM, element(obs.shape, 0)],
        flops=2**31,
    )


def final_step(plan, info, ints, later_ints, own, later, own_cov, later_cov, gains, inverse, moved, own_obs, later_obs):
    states, items, panel, width, number = plan.states, plan.items, plan.panel, plan.width, plan.number
    own_dyn, own_upper, own_small = own
    later_dyn, later_upper, later_small = later

    def body(
        info, ints, later_ints, own_dyn, own_upper, own_small, later_dyn, later_upper, later_small,
        own_cov, later_cov, gains, inverse, moved, own_obs, later_obs,
        out_dyn, out_off, out_cov, out_fac, out_info, weights, upper, held, fac,
    ):
        me = info[0]
        mine = pl.ds(pl.multiple_of(me * panel, panel), panel)
        tile = min(256, states)

        def columns(ref):
            if panel % 128 == 0:
                return jnp.transpose(ref[:, mine])
            return jnp.transpose(pltpu.roll(ref[...], states - me * panel, 1)[:, :panel])

        def own_row(ref):
            if panel % 128 == 0:
                return ref[:, mine]
            return pltpu.roll(ref[...], states - me * panel, 1)[:, :panel]

        fac[...] = dense_factor(own_obs[0], ints[0:1, :items], number)

        @pl.when(info[2] == 0)
        def _():
            out_dyn[0] = own_dyn[mine, :]
            out_off[0] = own_row(own_small)[0:1, :]
            out_cov[0] = own_cov[...]
            out_fac[0, :, :items] = columns(own_upper)
            out_fac[0, :, items : 2 * items] = columns(fac)
            out_fac[0, :, 2 * items :] = jnp.zeros((panel, 2 * items), F32)
            zeta = jnp.concatenate([own_small[1:2, :items], own_small[2:3, :items]], axis=1)
            zeta = jnp.broadcast_to(zeta, (SMALL, 2 * items))
            out_info[0] = mm(zeta, out_fac[0, :, : 2 * items], NT)[0:1, :]

        @pl.when(info[2] == 1)
        def _():
            inverse_pair = split(inverse[...])
            gains_pair = split(gains[...])
            factor = jnp.concatenate(
                [later_upper[...], dense_factor(later_obs[0], later_ints[0:1, :items], number)], axis=0
            )
            factor_pair = split(factor)

            def weigh(c, carry):
                at = pl.ds(pl.multiple_of(c * tile, tile), tile)
                weights[at, :] = dot3(split(dot3(split(later_dyn[at, :]), gains_pair, NN)), inverse_pair, NT)
                return carry

            lax.fori_loop(0, states // tile, weigh, 0)
            for a in range(plan.n):
                held[:, a * panel : (a + 1) * panel] = moved[a]
            own_weight = weights[mine, :]
            weight_pair = split(-own_weight)
            held_pair = split(held[...])
            cov_left = tuple(jnp.concatenate([a, b], axis=1) for a, b in zip(held_pair, weight_pair))
            dyn_pair = split(later_dyn[mine, :])
            left = tuple(jnp.concatenate([a, b], axis=1) for a, b in zip(dyn_pair, weight_pair))

            def finish(c, carry):
                at = pl.ds(pl.multiple_of(c * tile, tile), tile)
                own_pair = split(own_dyn[:, at])
                up = dot3(inverse_pair, split(dot3(factor_pair, own_pair, NN)), NN)
                upper[:, at] = up
                right = tuple(jnp.concatenate([a, b], axis=0) for a, b in zip(own_pair, split(up)))
                out_dyn[0, :, at] = dot3(left, right, NN)
                right = split(jnp.concatenate([later_dyn[at, :], weights[at, :]], axis=1))
                out_cov[0, :, at] = dot3(cov_left, right, NT) + later_cov[:, at]
                return carry

            lax.fori_loop(0, states // tile, finish, 0)
            residual = jnp.concatenate([later_small[1:2, :items], later_small[2:3, :items]], axis=1)
            offset = jnp.broadcast_to(own_small[0:1, :], (SMALL, states))
            residual = jnp.broadcast_to(residual, (SMALL, 2 * items)) - mm(offset, factor, NT)
            solved = mm(residual, inverse[...], NT)
            gone = mm(offset, later_dyn[mine, :], NT) + mm(solved, own_weight, NT)
            out_off[0] = gone[0:1, :] + own_row(later_small)[0:1, :]
            out_fac[0, :, : 2 * items] = columns(upper)
            out_fac[0, :, 2 * items : 3 * items] = columns(own_upper)
            out_fac[0, :, 3 * items :] = columns(fac)
            zeta = jnp.concatenate([solved[0:1, :], own_small[1:2, :items], own_small[2:3, :items]], axis=1)
            zeta = jnp.broadcast_to(zeta, (SMALL, 4 * items))
            out_info[0] = mm(zeta, out_fac[0], NT)[0:1, :]

    return call(
        body,
        "final",
        [
            (1, panel, states),
            (1, 1, panel),
            (1, panel, states),
            (1, panel, 4 * items),
            (1, 1, panel),
        ],
        (
            info, ints, later_ints, own_dyn, own_upper, own_small, later_dyn, later_upper, later_small,
            own_cov, later_cov, gains, inverse, moved, own_obs, later_obs,
        ),
        [SM] + [VM] * 13 + [element(own_obs.shape, 0), element(later_obs.shape, 0)],
        scratch=[
            pltpu.VMEM((states, 2 * items), F32),
            pltpu.VMEM((2 * items, states), F32),
            pltpu.VMEM((panel, states), F32),
            pltpu.VMEM((items, states), F32),
        ],
        flops=2**32,
    )


def per_device(mesh, dyn_pattern, dyn_values, offsets, covariance, obs_block, obs_matrix, obs_data):
    plan = Plan(mesh, dyn_pattern, dyn_values, obs_block, obs_matrix)
    here = lax.axis_index(PLANE)
    even_turn = 1 - lax.axis_index("tm") % 2
    info = jnp.stack([here, lax.axis_index("obs"), even_turn]).astype(jnp.int32)
    ints = jnp.concatenate([obs_block, dyn_pattern.reshape(2, -1)], axis=1)

    pieces = [obs_matrix] + [exchange(obs_matrix, "obs", k, plan.obs) for k in range(1, plan.obs)]
    message, obs = gain_step(plan, info, ints, pieces, covariance, offsets, obs_data)
    later_values = earlier(plan, dyn_values)
    own_even, own_odd = gather(plan, dyn_values)
    later_even, later_odd = gather(plan, later_values)
    gain_even, gain_odd = gather(plan, message)
    pack = system_step(plan, info, ints, gain_even, gain_odd, obs)
    later_ints = earlier(plan, ints)
    later_obs = earlier(plan, obs)
    later_pack = earlier(plan, pack)

    spread, values = spread_step(plan, info, ints, own_even, own_odd, covariance)
    moved = swap_blocks(plan, spread.reshape(plan.n, plan.panel, plan.panel))
    own_dyn, own_weights, own_upper, own_small = level_step(plan, ints, values, pack, obs)
    own_cov = covariance_step(plan, info, ints, moved, values, own_weights, covariance)
    later_cov = earlier(plan, own_cov)

    later_full = assemble_step(plan, info, later_even, later_odd)
    later_dyn, _, later_upper, later_small = level_step(plan, later_ints, later_full, later_pack, later_obs)
    gain = later_gain_step(plan, later_ints, own_cov, later_upper, later_obs)
    gain_even, gain_odd = gather(plan, gain)
    spread = later_spread_step(plan, later_dyn, own_cov)
    moved = swap_blocks(plan, spread.reshape(plan.n, plan.panel, plan.panel))
    gains, inverse = later_system_step(plan, info, later_ints, gain_even, gain_odd, later_upper, later_obs)
    dyn, off, cov, fac, information = final_step(
        plan, info, ints, later_ints,
        (own_dyn, own_upper, own_small), (later_dyn, later_upper, later_small),
        own_cov, later_cov, gains, inverse, moved, obs, later_obs,
    )
    return dyn, off[:, 0], cov, fac, information[:, 0]


def solution(mesh):
    placed = (
        P("tm", None, None),
        P("tm", PLANE, None),
        P("tm", PLANE),
        P("tm", PLANE, None),
        P("tm", None),
        P("tm", "obs", None),
        P("tm", "obs"),
    )

    def run(*arrays):
        return per_device(mesh, *arrays)

    return jax.shard_map(
        run,
        mesh=mesh,
        in_specs=placed,
        out_specs=(
            P("tm", PLANE, None),
            P("tm", PLANE),
            P("tm", PLANE, None),
            P("tm", PLANE, None),
            P("tm", PLANE),
        ),
        check_vma=False,
    )
```

```python
import jax
import jax.numpy as jnp
from jax import lax
from jax.experimental import pallas as pl
from jax.experimental.pallas import tpu as pltpu
from jax.sharding import PartitionSpec as P

F32 = jnp.float32
BF16 = jnp.bfloat16
NN = (((1,), (0,)), ((), ()))
NT = (((1,), (1,)), ((), ()))
PLANE = ("row", "obs")
SMALL = 8


def split(x):
    high = x.astype(BF16)
    return high, (x - high.astype(F32)).astype(BF16)


def dot3(left, right, dims):
    (a, b), (c, d) = left, right
    return lax.dot_general(
        jnp.concatenate([a, a, b], axis=1),
        jnp.concatenate([c, d, c], axis=dims[0][1][0]),
        dims,
        preferred_element_type=F32,
    )


def mm(left, right, dims=NN):
    return dot3(split(left), split(right), dims)


def reciprocal(x):
    y = pl.reciprocal(x, approx=True)
    return y * (2.0 - x * y)


def inverse_root(x):
    y = lax.rsqrt(x)
    return y * (1.5 - (0.5 * x) * (y * y))


def inverse_factor(matrix):
    size = matrix.shape[0]
    tiles = size // 8
    sub = lax.broadcasted_iota(jnp.int32, (8, size), 0)
    lane = lax.broadcasted_iota(jnp.int32, (8, size), 1)

    def wide(x):
        return jnp.broadcast_to(x, (8, size))

    rows = [matrix[8 * t : 8 * t + 8, :] for t in range(tiles)]
    inverse = [jnp.where(lane == sub + 8 * t, 1.0, 0.0).astype(F32) for t in range(tiles)]
    for p in range(tiles):
        column = {
            (t, c): wide(rows[t][:, 8 * p + c : 8 * p + c + 1])
            for t in range(p, tiles)
            for c in range(8)
        }
        scale = None
        for r in range(8):
            pivot = wide(column[p, r][r : r + 1, :])
            over = reciprocal(pivot)
            root = inverse_root(pivot)
            scale = root if r == 0 else jnp.where(sub == r, root, scale)
            factor = {t: column[t, r] * over for t in range(p, tiles)}
            for c in range(r + 1, 8):
                other = wide(column[p, r][c : c + 1, :])
                for t in range(p, tiles):
                    column[t, c] = column[t, c] - factor[t] * other
            factor[p] = jnp.where(sub > r, factor[p], 0.0)
            row_here = wide(rows[p][r : r + 1, :])
            inverse_here = wide(inverse[p][r : r + 1, :])
            for t in range(p, tiles):
                rows[t] = rows[t] - factor[t] * row_here
                inverse[t] = inverse[t] - factor[t] * inverse_here
        inverse[p] = inverse[p] * scale
    return jnp.concatenate(inverse, axis=0)


def identity(size):
    sub = lax.broadcasted_iota(jnp.int32, (size, size), 0)
    lane = lax.broadcasted_iota(jnp.int32, (size, size), 1)
    return jnp.where(sub == lane, 1.0, 0.0).astype(F32)


def dense_factor(matrix, blocks, number):
    items, width = matrix.shape[0], matrix.shape[1] // 2
    at = jnp.transpose(jnp.broadcast_to(blocks.astype(F32), (width, items)))
    pieces = []
    for r in range(number):
        first = jnp.where(at == float(r), matrix[:, :width], 0.0)
        second = jnp.where(at == float((r - 1) % number), matrix[:, width:], 0.0)
        pieces.append(first + second)
    return jnp.concatenate(pieces, axis=1)


def call(body, name, out_shapes, args, specs, scratch=(), micros=1, grant=24):
    return pl.pallas_call(
        body,
        name=name,
        grid=(1,),
        in_specs=specs,
        out_specs=[VM] * len(out_shapes),
        out_shape=[s if isinstance(s, jax.ShapeDtypeStruct) else jax.ShapeDtypeStruct(s, F32) for s in out_shapes],
        scratch_shapes=list(scratch),
        compiler_params=pltpu.CompilerParams(vmem_limit_bytes=grant * 2**20),
        cost_estimate=pl.CostEstimate(flops=micros * 10**9, bytes_accessed=2**20, transcendentals=0),
    )(*args)


VM = pl.BlockSpec(memory_space=pltpu.VMEM)
SM = pl.BlockSpec(memory_space=pltpu.SMEM)


def element(shape, which):
    return pl.BlockSpec((1,) + tuple(shape[1:]), lambda i: (which,) + (0,) * (len(shape) - 1))


def part(shape, which):
    if len(shape) == 3:
        return VM
    return pl.BlockSpec((shape[0], None) + tuple(shape[2:]), lambda i: (0, which, 0, 0))


class Plan:
    def __init__(self, mesh, pattern, values, obs_block, obs_matrix):
        self.row, self.obs = mesh.shape["row"], mesh.shape["obs"]
        self.tm = mesh.shape["tm"]
        self.n = self.row * self.obs
        self.number, self.per_row = pattern.shape[1:]
        self.panel = values.shape[1]
        self.states = self.panel * self.n
        self.width = self.states // self.number
        self.items = obs_block.shape[1]
        self.share = obs_matrix.shape[1]
        self.swapped = self.n == 8 and self.panel % 128 == 0

    def source(self, info, k):
        return lax.bitwise_xor(info[0], k) if self.swapped else k

    def rows_of(self, info, k):
        start = self.source(info, k) * self.panel
        return pl.ds(pl.multiple_of(start, self.panel) if self.swapped else start, self.panel)


def exchange(x, axes, mask, size):
    return lax.ppermute(x, axes, [(a, a ^ mask) for a in range(size)])


def first_leg(plan, x):
    if plan.swapped:
        return [x] + [exchange(x, PLANE, k, plan.n) for k in (2, 4, 6)]
    return [lax.all_gather(x, PLANE, axis=0)]


def second_leg(plan, pieces):
    if plan.swapped:
        even = jnp.stack(pieces)
        return even, exchange(even, PLANE, 1, plan.n)
    return pieces[0][0::2], pieces[0][1::2]


def other_core(plan, even, odd):
    if plan.swapped:
        return exchange(even, PLANE, 1, plan.n)
    return earlier(plan, odd)


def gather(plan, x):
    return second_leg(plan, first_leg(plan, x))


def tie(*trees):
    return lax.optimization_barrier(trees)


def swap_blocks(plan, x):
    return lax.all_to_all(x, PLANE, 0, 0, tiled=True)


def earlier(plan, x):
    return lax.ppermute(x, "tm", [(i, i - 1) for i in range(1, plan.tm)])


def gain_step(plan, info, blocks, pieces, covariance, offsets, data):
    share, panel, items = plan.share, plan.panel, plan.items

    def body(info, blocks, *refs):
        parts = refs[: plan.obs]
        cov, off, dat, message, obs = refs[plan.obs :]
        for k, part in enumerate(parts):
            start = pl.multiple_of(lax.bitwise_xor(info[1], k) * share, share)
            obs[:, pl.ds(start, share), :] = part[...]
        factor = dense_factor(obs[1], blocks[1:2, :], plan.number)
        message[:panel, :] = mm(cov[0], factor, NT)
        message[panel:, :] = jnp.zeros((SMALL, items), F32)
        message[panel : panel + 2, :panel] = off[...]
        spread = jnp.concatenate([dat[...], jnp.zeros((2, items - share), F32)], axis=1)
        spread = jnp.concatenate([spread, jnp.zeros((6, items), F32)], axis=0)
        message[panel + 2 : panel + 4, :] = pltpu.roll(spread, info[1] * share, 1)[:2]

    return call(
        body,
        "gain",
        [(panel + SMALL, items), (2, items, 2 * plan.width)],
        (info, blocks, *pieces, covariance, offsets, data),
        [SM, VM] + [VM] * plan.obs + [element(covariance.shape, 0), VM, VM],
        grant=56,
        micros=1,
    )


def system_step(plan, info, ints, even, odd, obs):
    states, items, panel = plan.states, plan.items, plan.panel

    def body(info, ints, even, odd, obs, gains, pack):
        tail = items
        zeta = jnp.zeros((2, items), F32)
        end = tail + SMALL * plan.number
        pack[tail:end, :] = jnp.zeros((SMALL * plan.number, items), F32)
        for e in range(2):
            for h in range(2):
                at = end + (2 * e + h) * items
                pack[at : at + items, :] = obs[e, :, h * plan.width : (h + 1) * plan.width]
        for k in range(plan.n):
            piece = (even, odd)[k % 2]
            gains[plan.rows_of(info, k), :] = piece[k // 2, :panel, :]
            start = plan.source(info, k) * panel
            if plan.swapped:
                block = start // plan.width
                at = pl.multiple_of(tail + block * SMALL, SMALL)
                pack[pl.ds(at, 2), :] = piece[k // 2, panel : panel + 2, :]
            else:
                at = tail + start // plan.width * SMALL
                lane = start % plan.width
                pack[at : at + 2, lane : lane + panel] = piece[k // 2, panel : panel + 2, :panel]
            if k < plan.obs:
                zeta = zeta + piece[k // 2, panel + 2 : panel + 4, :]
        pack[tail + 2 : tail + 4, :] = zeta
        factor = dense_factor(obs[1], ints[1:2, :items], plan.number)
        system = identity(items) + mm(factor, gains[...])
        pack[:tail, :] = inverse_factor(system)

    return call(
        body,
        "system",
        [(states, items), (5 * items + SMALL * plan.number, items)],
        (info, ints, even, odd, obs),
        [SM, VM, VM, VM, VM],
        micros=20,
    )


def fill(plan, info, even, odd, out):
    for k in range(plan.n):
        out[plan.rows_of(info, k), :] = (even, odd)[k % 2][k // 2, : plan.panel]


def starts(plan, ints, which, c):
    return [
        pl.multiple_of(ints[which, plan.items + c * plan.per_row + k] * plan.width, plan.width)
        for k in range(plan.per_row)
    ]


def spread_step(plan, info, ints, even, odd, covariance):
    states, panel, width = plan.states, plan.panel, plan.width
    wide = plan.per_row * width

    def body(info, ints, even, odd, cov, out, values, high, low):
        fill(plan, info, even, odd, values)
        high[...], low[...] = split(cov[0])
        for c in range(plan.number):
            taken = tuple(
                jnp.concatenate([r[:, pl.ds(s, width)] for s in starts(plan, ints, 1, c)], axis=1)
                for r in (high, low)
            )
            at = slice(c * width, (c + 1) * width)
            out[at, :] = dot3(split(values[at, :]), taken, NT)

    return call(
        body,
        "spread",
        [(states, panel), (states, wide)],
        (info, ints, even, odd, covariance),
        [SM, SM, VM, VM, element(covariance.shape, 0)],
        scratch=[pltpu.VMEM((panel, states), BF16)] * 2,
        micros=1,
    )


def packed_factor(plan, ints, which, pack):
    at = plan.items + SMALL * plan.number + 2 * which * plan.items
    matrix = jnp.concatenate([pack[at + h * plan.items : at + (h + 1) * plan.items, :] for h in range(2)], axis=1)
    return dense_factor(matrix, ints[which : which + 1, : plan.items], plan.number)


def gathered(plan, ints, which, c, refs):
    begins = starts(plan, ints, which, c)
    return tuple(jnp.concatenate([r[pl.ds(s, plan.width), :] for s in begins], axis=0) for r in refs)


def gathered_columns(plan, ints, which, c, refs):
    begins = starts(plan, ints, which, c)
    return tuple(jnp.concatenate([r[:, pl.ds(s, plan.width)] for s in begins], axis=1) for r in refs)


def block(plan, c):
    return slice(c * plan.width, (c + 1) * plan.width)


def beside(first, second, axis):
    return tuple(jnp.concatenate([x, y], axis=axis) for x, y in zip(first, second))


def negative(pair):
    return tuple(-x for x in pair)


def across(plan, ints, which, left, values, out, rows=None):
    if rows is None:
        rows = range(plan.number)
    width = plan.width
    out[...] = jnp.zeros_like(out)
    for i, c in enumerate(rows):
        product = dot3(left(i, c), split(values(c)), NN)
        for k, s in enumerate(starts(plan, ints, which, c)):
            at = pl.ds(s, width)
            out[:, at] = out[:, at] + product[:, k * width : (k + 1) * width]


def columns_of(pair, at):
    return tuple(x[:, at] for x in pair)


def upper_part(plan, ints, factor, inverse, values, upper, seen):
    pair = split(factor)
    across(plan, ints, 0, lambda i, c: columns_of(pair, block(plan, c)), lambda c: values[block(plan, c), :], seen)
    upper[...] = dot3(inverse, split(seen[...]), NN)


def weigh(plan, ints, values, gains, pack, gain_h, gain_l, weights):
    items = plan.items
    inverse = split(pack[:items, :])
    gain_h[...], gain_l[...] = split(dot3(split(gains), inverse, NT))
    for c in range(plan.number):
        weights[block(plan, c), :] = dot3(
            split(values[block(plan, c), :]), gathered(plan, ints, 1, c, (gain_h, gain_l)), NN
        )


def solve_vectors(plan, pack, factor, small):
    items, number = plan.items, plan.number
    tail = items
    vector = jnp.concatenate(
        [pack[tail + c * SMALL : tail + (c + 1) * SMALL, :] for c in range(number)], axis=1
    )
    zeta = pack[tail : tail + SMALL, :]
    residual = zeta[3:4, :] - mm(vector, factor, NT)[0:1, :]
    solved = mm(jnp.broadcast_to(residual, (SMALL, items)), pack[:tail, :], NT)
    small[0:1, :] = solved[0:1, :]
    small[1:2, :] = zeta[2:3, :]
    small[2:, :] = jnp.zeros((SMALL - 2, items), F32)
    return solved


def earlier_offsets(plan, ints, c, pack):
    tail = plan.items
    begins = [
        pl.multiple_of(tail + ints[1, plan.items + c * plan.per_row + k] * SMALL, SMALL)
        for k in range(plan.per_row)
    ]
    return [pack[pl.ds(s, SMALL), :] for s in begins]


def own_block(plan, info):
    start = info[0] * plan.panel
    return start // plan.width, pl.ds(pl.multiple_of(start, plan.panel), plan.panel)


def panel_dynamics(plan, info, ints, first, second, weights, upper_pair, out):
    width = plan.width
    c, mine = own_block(plan, info)
    left = split(second[mine, :])
    middle = [ints[1, plan.items + c * plan.per_row + k] for k in range(plan.per_row)]
    across(
        plan,
        ints,
        0,
        lambda i, c: columns_of(left, slice(i * width, (i + 1) * width)),
        lambda c: first[pl.ds(pl.multiple_of(c * width, width), width), :],
        out,
        middle,
    )
    out[...] = out[...] - dot3(split(weights[mine, :]), upper_pair, NN)


def level_step(plan, info, ints, even, odd, values, gains, pack):
    states, items = plan.states, plan.items

    def body(info, ints, ints_v, even, odd, values, gains, pack, first, weights, upper, small, *scratch):
        seen, gain_h, gain_l = scratch
        fill(plan, info, even, odd, first)
        factor = packed_factor(plan, ints_v, 1, pack)
        inverse = split(pack[:items, :])
        upper_part(plan, ints, factor, inverse, first, upper, seen)
        weigh(plan, ints, values, gains[...], pack, gain_h, gain_l, weights)
        solve_vectors(plan, pack, factor, small)

    return call(
        body,
        "level",
        [(states, plan.per_row * plan.width), (states, items), (items, states), (SMALL, items)],
        (info, ints, ints, even, odd, values, gains, pack),
        [SM, SM, VM, VM, VM, VM, VM, VM],
        scratch=[pltpu.VMEM((items, states), F32)] + [pltpu.VMEM((states, items), BF16)] * 2,
        micros=1,
    )


def later_upper_step(plan, info, ints, even, odd, pack):
    states, items = plan.states, plan.items

    def body(info, ints, ints_v, even, odd, pack, first, upper, seen):
        fill(plan, info, even, odd, first)
        factor = packed_factor(plan, ints_v, 1, pack)
        inverse = split(pack[:items, :])
        upper_part(plan, ints, factor, inverse, first, upper, seen)

    return call(
        body,
        "later_upper",
        [(states, plan.per_row * plan.width), (items, states)],
        (info, ints, ints, even, odd, pack),
        [SM, SM, VM, part(even.shape, 0), part(odd.shape, 0), VM],
        scratch=[pltpu.VMEM((items, states), F32)],
        micros=1,
    )


def later_level_step(plan, info, ints, even, odd, gain_even, gain_odd, first, upper, pack, cov):
    states, items, panel = plan.states, plan.items, plan.panel

    def body(info, ints, ints_v, even, odd, gain_even, gain_odd, first, upper, pack, cov, second, weights, small, out, dyn, offset, *scratch):
        gains, gain_h, gain_l, cov_h, cov_l, part_h, part_l = scratch
        fill(plan, info, even, odd, second)
        fill(plan, info, gain_even, gain_odd, gains)
        weigh(plan, ints, second, gains[...], pack, gain_h, gain_l, weights)
        cov_h[...], cov_l[...] = split(cov[...])
        upper_pair = split(upper[...])
        rest = split(dot3(upper_pair, (cov_h[...], cov_l[...]), NT))
        for c in range(plan.number):
            at = block(plan, c)
            taken = gathered_columns(plan, ints, 0, c, (cov_h, cov_l))
            part_h[at, :], part_l[at, :] = split(dot3(split(first[at, :]), taken, NT))
        for c in range(plan.number):
            at = block(plan, c)
            left = beside(split(second[at, :]), negative(split(weights[at, :])), 1)
            out[at, :] = dot3(left, beside(gathered(plan, ints, 1, c, (part_h, part_l)), rest, 0), NN)
        panel_dynamics(plan, info, ints, first, second, weights, upper_pair, dyn)
        factor = packed_factor(plan, ints_v, 1, pack)
        solved = solve_vectors(plan, pack, factor, small)
        c, mine = own_block(plan, info)
        left = jnp.concatenate(earlier_offsets(plan, ints, c, pack) + [solved], axis=1)
        right = jnp.concatenate([second[mine, :], weights[mine, :]], axis=1)
        own = pack[pl.ds(pl.multiple_of(items + c * SMALL, SMALL), SMALL), :]
        if panel % plan.width:
            own = pltpu.roll(own, plan.width - lax.rem(info[0] * panel, plan.width), 1)[:, :panel]
        offset[...] = mm(left, right, NT) + jnp.broadcast_to(own[1:2, :], (SMALL, panel))

    return call(
        body,
        "later_level",
        [
            (states, plan.per_row * plan.width),
            (states, items),
            (SMALL, items),
            (states, panel),
            (panel, states),
            (SMALL, panel),
        ],
        (info, ints, ints, even, odd, gain_even, gain_odd, first, upper, pack, cov),
        [SM, SM, VM, part(even.shape, 1), part(odd.shape, 1), VM, VM, VM, VM, VM, VM],
        scratch=[pltpu.VMEM((states, items), F32)]
        + [pltpu.VMEM((states, items), BF16)] * 2
        + [pltpu.VMEM((panel, states), BF16)] * 2
        + [pltpu.VMEM((states, panel), BF16)] * 2,
        micros=1,
    )


def ahead_step(plan, info, ints, later_ints, first, second, weights, upper, later_upper, later_pack):
    states, items, panel, width = plan.states, plan.items, plan.panel, plan.width

    def body(info, ints, ints_v, first, second, weights, upper, later_upper, pack, out, column, high, low):
        c, _ = own_block(plan, info)
        for r in range(plan.number):
            total = jnp.zeros((width, width), F32)
            for k in range(plan.per_row):
                here = ints[0, items + r * plan.per_row + k] == c
                total = total + jnp.where(here, first[block(plan, r), k * width : (k + 1) * width], 0.0)
            if panel % width:
                total = pltpu.roll(total, width - lax.rem(info[0] * panel, width), 1)
            column[block(plan, r), :] = total[:, :panel]
        high[...], low[...] = split(column[...])
        if panel % width:
            shift = states - info[0] * panel
            rest = split(pltpu.roll(upper[...], shift, 1)[:, :panel])
        else:
            rest = split(upper[:, own_block(plan, info)[1]])
        for r in range(plan.number):
            at = block(plan, r)
            left = beside(split(second[at, :]), negative(split(weights[at, :])), 1)
            column[at, :] = dot3(left, beside(gathered(plan, ints, 1, r, (high, low)), rest, 0), NN)
        factor = jnp.concatenate(
            [later_upper[...], packed_factor(plan, ints_v, 0, pack)], axis=0
        )
        out[...] = mm(factor, column[...], NN)

    return call(
        body,
        "ahead",
        [(2 * items, panel)],
        (info, ints, later_ints, first, second, weights, upper, later_upper, later_pack),
        [SM, SM, VM, VM, VM, VM, VM, VM, VM],
        scratch=[pltpu.VMEM((states, panel), F32)] + [pltpu.VMEM((states, panel), BF16)] * 2,
        micros=1,
    )[0]


def covariance_step(plan, info, ints, moved, values, weights, covariance, pack, small):
    states, panel, items = plan.states, plan.panel, plan.items
    tail = items

    def body(info, ints, moved, values, weights, cov, pack, small, out, offset, held_h, held_l):
        for a in range(plan.n):
            at = slice(a * panel, (a + 1) * panel)
            held_h[:, at], held_l[:, at] = split(moved[a])
        mine = own_block(plan, info)[1]
        solved = jnp.broadcast_to(small[0:1, :], (SMALL, items))
        last = split(jnp.concatenate([-weights[mine, :], solved], axis=0))
        for c in range(plan.number):
            at = block(plan, c)
            top = gathered_columns(plan, ints, 1, c, (held_h, held_l))
            low = split(jnp.concatenate(earlier_offsets(plan, ints, c, pack), axis=1))
            left = beside(beside(top, low, 0), last, 1)
            right = beside(split(values[at, :]), split(weights[at, :]), 1)
            result = dot3(left, right, NT)
            out[:, at] = result[:panel, :] + cov[0, :, at]
            own = pack[tail + c * SMALL : tail + (c + 1) * SMALL, :]
            offset[:, at] = result[panel:, :] + jnp.broadcast_to(own[1:2, :], (SMALL, items))

    return call(
        body,
        "covariance",
        [(panel, states), (SMALL, states)],
        (info, ints, moved, values, weights, covariance, pack, small),
        [SM, SM, VM, VM, VM, element(covariance.shape, 1), VM, VM],
        scratch=[pltpu.VMEM((panel, states), BF16)] * 2,
        grant=56,
        micros=1,
    )


def later_gain_step(plan, ints, cov, upper, pack):
    items = plan.items

    def body(ints, cov, upper, pack, out):
        factor = jnp.concatenate([upper[...], packed_factor(plan, ints, 0, pack)], axis=0)
        out[...] = mm(cov[...], factor, NT)

    return call(
        body,
        "later_gain",
        [(plan.panel, 2 * items)],
        (ints, cov, upper, pack),
        [VM, VM, VM, VM],
        micros=1,
    )[0]


def later_system_step(plan, info, ints, even, odd, upper, pack, first, second, weights):
    states, items = plan.states, plan.items
    rank = 2 * items

    def body(info, ints, ints_v, even, odd, upper, pack, first, second, weights, carried, inverse, *scratch):
        gain_h, gain_l, part_h, part_l = scratch
        for k in range(plan.n):
            at = plan.rows_of(info, k)
            gain_h[at, :], gain_l[at, :] = split((even, odd)[k % 2][k // 2])
        pair = (gain_h[...], gain_l[...])
        above = dot3(split(upper[...]), pair, NN)
        other = packed_factor(plan, ints_v, 0, pack)
        below = dot3(split(other), pair, NN)
        for c in range(plan.number):
            at = block(plan, c)
            taken = gathered(plan, ints, 0, c, (gain_h, gain_l))
            part_h[at, :], part_l[at, :] = split(dot3(split(first[at, :]), taken, NN))
        rest = split(above)
        for c in range(plan.number):
            at = block(plan, c)
            left = beside(split(second[at, :]), negative(split(weights[at, :])), 1)
            carried[at, :] = dot3(left, beside(gathered(plan, ints, 1, c, (part_h, part_l)), rest, 0), NN)
        top = inverse_factor(identity(items) + above[:, :items])
        lower = mm(below[:, :items], top, NT)
        bottom = inverse_factor(identity(items) + below[:, items:] - mm(lower, lower, NT))
        inverse[:items, :items] = top
        inverse[:items, items:] = jnp.zeros((items, items), F32)
        inverse[items:, :items] = -mm(bottom, mm(lower, top))
        inverse[items:, items:] = bottom

    return call(
        body,
        "later_system",
        [(states, rank), (rank, rank)],
        (info, ints, ints, even, odd, upper, pack, first, second, weights),
        [SM, SM, VM, VM, VM, VM, VM, VM, VM, VM],
        scratch=[pltpu.VMEM((states, rank), BF16)] * 4,
        grant=56,
        micros=15,
    )


def final_step(plan, info, ints, later_ints, own, later, covs, carried, inverse, moved, seen, pack, later_pack):
    states, items, panel, width, number = plan.states, plan.items, plan.panel, plan.width, plan.number
    rank = 2 * items

    def body(
        info, ints, later_ints, ints_v, later_ints_v,
        first, second, own_weights, own_upper, own_small, own_offset,
        later_first, later_second, later_weights, later_upper, later_small, later_dyn, later_offset,
        own_cov, later_cov, carried, inverse, moved, seen, pack, later_pack,
        out_dyn, out_off, out_cov, out_fac, out_info,
        weights, fac, held_h, held_l, part_h, part_l, dyn, half,
    ):
        mine = own_block(plan, info)[1]

        def own_columns(ref):
            if panel % 128 == 0:
                return ref[:, mine]
            return pltpu.roll(ref[...], states - info[0] * panel, 1)[:, :panel]

        fac[...] = packed_factor(plan, ints_v, 0, pack)
        last = [jnp.transpose(own_columns(own_upper)), jnp.transpose(own_columns(fac))]

        @pl.when(info[2] == 0)
        def _():
            panel_dynamics(plan, info, ints, first, second, own_weights, split(own_upper[...]), dyn)
            out_dyn[0] = dyn[...]
            out_off[0] = own_columns(own_offset)[0:1, :]
            out_cov[0] = own_cov[...]
            out_fac[0, :, :items] = last[0]
            out_fac[0, :, items:rank] = last[1]
            out_fac[0, :, rank:] = jnp.zeros((panel, rank), F32)
            zeta = jnp.concatenate([own_small[0:1, :], own_small[1:2, :]], axis=1)
            zeta = jnp.broadcast_to(zeta, (SMALL, rank))
            out_info[0] = mm(zeta, out_fac[0, :, :rank], NT)[0:1, :]

        @pl.when(info[2] == 1)
        def _():
            inverse_pair = split(inverse[...])
            weights[...] = dot3(split(carried[...]), inverse_pair, NT)
            own_weight = weights[mine, :]
            weight_pair = split(-own_weight)
            factor = jnp.concatenate(
                [later_upper[...], packed_factor(plan, later_ints_v, 0, later_pack)], axis=0
            )
            factor_pair = split(factor)
            left = later_dyn[...] + dot3(split(dot3(weight_pair, inverse_pair, NN)), factor_pair, NN)
            left_pair = split(left)
            across(
                plan, ints, 1, lambda i, c: columns_of(left_pair, block(plan, c)),
                lambda c: second[block(plan, c), :], half,
            )
            for a in range(plan.n):
                at = slice(a * panel, (a + 1) * panel)
                held_h[:, at], held_l[:, at] = split(moved[a])
            rest = negative(split(dot3((held_h[...], held_l[...]), split(later_upper[...]), NT)))
            for c in range(number):
                at = block(plan, c)
                taken = gathered_columns(plan, later_ints, 0, c, (held_h, held_l))
                part_h[:, at], part_l[:, at] = split(dot3(taken, split(later_first[at, :]), NT))
            rest = beside(rest, weight_pair, 1)
            middle = split(half[...])
            across(
                plan, ints, 0, lambda i, c: columns_of(middle, block(plan, c)),
                lambda c: first[block(plan, c), :], dyn,
            )
            for c in range(number):
                at = block(plan, c)
                taken = beside(gathered_columns(plan, later_ints, 1, c, (part_h, part_l)), rest, 1)
                right = jnp.concatenate([later_second[at, :], later_weights[at, :], weights[at, :]], axis=1)
                out_cov[0, :, at] = dot3(taken, split(right), NT) + later_cov[:, at]
            through = split(dot3(left_pair, split(own_weights[...]), NN))
            out_dyn[0] = dyn[...] - dot3(through, split(own_upper[...]), NN)
            residual = jnp.concatenate([later_small[0:1, :], later_small[1:2, :]], axis=1)
            offset = own_offset[...]
            residual = jnp.broadcast_to(residual, (SMALL, rank)) - dot3(split(offset), factor_pair, NT)
            solved = dot3(split(residual), inverse_pair, NT)
            gone = mm(offset, later_dyn[...], NT) + mm(solved, own_weight, NT)
            out_off[0] = gone[0:1, :] + later_offset[0:1, :]
            out_fac[0, :, :rank] = jnp.transpose(dot3(inverse_pair, split(seen[...]), NN))
            out_fac[0, :, rank : rank + items] = last[0]
            out_fac[0, :, rank + items :] = last[1]
            zeta = jnp.concatenate([solved[0:1, :], own_small[0:1, :], own_small[1:2, :]], axis=1)
            zeta = jnp.broadcast_to(zeta, (SMALL, 2 * rank))
            out_info[0] = mm(zeta, out_fac[0], NT)[0:1, :]

    return call(
        body,
        "final",
        [
            (1, panel, states),
            (1, 1, panel),
            (1, panel, states),
            (1, panel, 2 * rank),
            (1, 1, panel),
        ],
        (
            info, ints, later_ints, ints, later_ints, *own, *later, *covs,
            carried, inverse, moved, seen, pack, later_pack,
        ),
        [SM] * 3 + [VM] * 21 + [VM, VM],
        scratch=[
            pltpu.VMEM((states, rank), F32),
            pltpu.VMEM((items, states), F32),
        ]
        + [pltpu.VMEM((panel, states), BF16)] * 4
        + [pltpu.VMEM((panel, states), F32)] * 2,
        grant=56,
        micros=1,
    )


def per_device(mesh, dyn_pattern, dyn_values, offsets, covariance, obs_block, obs_matrix, obs_data):
    plan = Plan(mesh, dyn_pattern, dyn_values, obs_block, obs_matrix)
    here = lax.axis_index(PLANE)
    even_turn = 1 - lax.axis_index("tm") % 2
    info = jnp.stack([here, lax.axis_index("obs"), even_turn]).astype(jnp.int32)
    ints = jnp.concatenate([obs_block, dyn_pattern.reshape(2, -1)], axis=1)

    pieces = [obs_matrix] + [exchange(obs_matrix, "obs", k, plan.obs) for k in range(1, plan.obs)]
    later_ints = earlier(plan, ints)
    own_first, own_second = dyn_values[0], dyn_values[1]
    pieces, own_first, own_second = tie(pieces, own_first, own_second)
    later_values = earlier(plan, own_first)
    message, obs = gain_step(plan, info, obs_block, pieces, covariance, offsets, obs_data)
    gain_leg_one = first_leg(plan, message)
    gain_leg_one, own_second, own_first, later_ints = tie(gain_leg_one, own_second, own_first, later_ints)
    gain_even, gain_odd = second_leg(plan, gain_leg_one)
    later_gain_even = earlier(plan, gain_even)
    second_leg_one = first_leg(plan, own_second)
    gains, pack = system_step(plan, info, ints, gain_even, gain_odd, obs)
    pack, second_leg_one, own_first, later_values, later_gain_even = tie(
        pack, second_leg_one, own_first, later_values, later_gain_even
    )
    later_pack = earlier(plan, pack)
    second_even, second_odd = second_leg(plan, second_leg_one)
    later_second_even = earlier(plan, second_even)
    first_leg_one = first_leg(plan, own_first)

    spread, second = spread_step(plan, info, ints, second_even, second_odd, covariance)
    first_leg_one, second, later_values, later_pack, later_gain_even = tie(
        first_leg_one, second, later_values, later_pack, later_gain_even
    )
    moved = swap_blocks(plan, spread.reshape(plan.n, plan.panel, plan.panel))
    first_even, first_odd = second_leg(plan, first_leg_one)
    later_leg_one = first_leg(plan, later_values)
    later_gain_odd = other_core(plan, later_gain_even, gain_odd)
    first, weights, upper, small = level_step(plan, info, ints, first_even, first_odd, second, gains, pack)
    moved, weights, later_leg_one, later_second_even = tie(moved, weights, later_leg_one, later_second_even)
    later_even, later_odd = second_leg(plan, later_leg_one)
    later_second_odd = other_core(plan, later_second_even, second_odd)
    cov, offset = covariance_step(plan, info, ints, moved, second, weights, covariance, pack, small)
    own = (first, second, weights, upper, small, offset)

    later_first, later_upper = later_upper_step(plan, info, later_ints, later_even, later_odd, later_pack)
    gain = later_gain_step(plan, later_ints, cov, later_upper, later_pack)
    gain_leg_one = first_leg(plan, gain)
    later_second, later_weights, later_small, spread, later_dyn, later_offset = later_level_step(
        plan, info, later_ints, later_second_even, later_second_odd, later_gain_even, later_gain_odd,
        later_first, later_upper, later_pack, cov,
    )
    gain_leg_one, spread, cov = tie(gain_leg_one, spread, cov)
    later_cov = earlier(plan, cov)
    later = (later_first, later_second, later_weights, later_upper, later_small, later_dyn, later_offset)
    gain_even, gain_odd = second_leg(plan, gain_leg_one)
    moved = swap_blocks(plan, spread.reshape(plan.n, plan.panel, plan.panel))
    seen = ahead_step(plan, info, ints, later_ints, first, second, weights, upper, later_upper, later_pack)
    carried, inverse = later_system_step(
        plan, info, later_ints, gain_even, gain_odd, later_upper, later_pack,
        later_first, later_second, later_weights,
    )
    moved, later_cov, inverse = tie(moved, later_cov, inverse)
    dyn, off, cov, fac, information = final_step(
        plan, info, ints, later_ints, own, later, (cov, later_cov), carried, inverse, moved, seen, pack, later_pack
    )
    return dyn, off[:, 0], cov, fac, information[:, 0]


def solution(mesh):
    placed = (
        P("tm", None, None),
        P("tm", PLANE, None),
        P("tm", PLANE),
        P("tm", PLANE, None),
        P("tm", None),
        P("tm", "obs", None),
        P("tm", "obs"),
    )

    def run(*arrays):
        return per_device(mesh, *arrays)

    return jax.shard_map(
        run,
        mesh=mesh,
        in_specs=placed,
        out_specs=(
            P("tm", PLANE, None),
            P("tm", PLANE),
            P("tm", PLANE, None),
            P("tm", PLANE, None),
            P("tm", PLANE),
        ),
        check_vma=False,
    )
```

```python
import jax
import jax.numpy as jnp
from jax import lax
from jax.experimental import pallas as pl
from jax.experimental.pallas import tpu as pltpu
from jax.sharding import PartitionSpec as P

F32 = jnp.float32
BF16 = jnp.bfloat16
NN = (((1,), (0,)), ((), ()))
NT = (((1,), (1,)), ((), ()))
PLANE = ("row", "obs")
SMALL = 8


def split(x):
    high = x.astype(BF16)
    return high, (x - high.astype(F32)).astype(BF16)


def dot3(left, right, dims):
    (a, b), (c, d) = left, right
    return lax.dot_general(
        jnp.concatenate([a, a, b], axis=1),
        jnp.concatenate([c, d, c], axis=dims[0][1][0]),
        dims,
        preferred_element_type=F32,
    )


def mm(left, right, dims=NN):
    return dot3(split(left), split(right), dims)


def reciprocal(x):
    y = pl.reciprocal(x, approx=True)
    return y * (2.0 - x * y)


def inverse_root(x):
    y = lax.rsqrt(x)
    return y * (1.5 - (0.5 * x) * (y * y))


def inverse_factor(matrix):
    size = matrix.shape[0]
    tiles = size // 8
    sub = lax.broadcasted_iota(jnp.int32, (8, size), 0)
    lane = lax.broadcasted_iota(jnp.int32, (8, size), 1)

    def wide(x):
        return jnp.broadcast_to(x, (8, size))

    rows = [matrix[8 * t : 8 * t + 8, :] for t in range(tiles)]
    inverse = [jnp.where(lane == sub + 8 * t, 1.0, 0.0).astype(F32) for t in range(tiles)]
    for p in range(tiles):
        column = {
            (t, c): wide(rows[t][:, 8 * p + c : 8 * p + c + 1])
            for t in range(p, tiles)
            for c in range(8)
        }
        scale = None
        for r in range(8):
            pivot = wide(column[p, r][r : r + 1, :])
            over = reciprocal(pivot)
            root = inverse_root(pivot)
            scale = root if r == 0 else jnp.where(sub == r, root, scale)
            factor = {t: column[t, r] * over for t in range(p, tiles)}
            for c in range(r + 1, 8):
                other = wide(column[p, r][c : c + 1, :])
                for t in range(p, tiles):
                    column[t, c] = column[t, c] - factor[t] * other
            factor[p] = jnp.where(sub > r, factor[p], 0.0)
            row_here = wide(rows[p][r : r + 1, :])
            inverse_here = wide(inverse[p][r : r + 1, :])
            for t in range(p, tiles):
                rows[t] = rows[t] - factor[t] * row_here
                inverse[t] = inverse[t] - factor[t] * inverse_here
        inverse[p] = inverse[p] * scale
    return jnp.concatenate(inverse, axis=0)


def identity(size):
    sub = lax.broadcasted_iota(jnp.int32, (size, size), 0)
    lane = lax.broadcasted_iota(jnp.int32, (size, size), 1)
    return jnp.where(sub == lane, 1.0, 0.0).astype(F32)


def dense_factor(matrix, blocks, number):
    items, width = matrix.shape[0], matrix.shape[1] // 2
    at = jnp.transpose(jnp.broadcast_to(blocks.astype(F32), (width, items)))
    pieces = []
    for r in range(number):
        first = jnp.where(at == float(r), matrix[:, :width], 0.0)
        second = jnp.where(at == float((r - 1) % number), matrix[:, width:], 0.0)
        pieces.append(first + second)
    return jnp.concatenate(pieces, axis=1)


def call(body, name, out_shapes, args, specs, scratch=(), micros=1, grant=24):
    return pl.pallas_call(
        body,
        name=name,
        grid=(1,),
        in_specs=specs,
        out_specs=[VM] * len(out_shapes),
        out_shape=[s if isinstance(s, jax.ShapeDtypeStruct) else jax.ShapeDtypeStruct(s, F32) for s in out_shapes],
        scratch_shapes=list(scratch),
        compiler_params=pltpu.CompilerParams(vmem_limit_bytes=grant * 2**20),
        cost_estimate=pl.CostEstimate(flops=micros * 10**9, bytes_accessed=2**20, transcendentals=0),
    )(*args)


def lazy(count, body):
    def run(inputs, *refs):
        sources = refs[inputs - count : inputs]
        held = refs[len(refs) - count - 1 : len(refs) - 1]
        sems = refs[-1]
        copies = [pltpu.make_async_copy(a, b, sems.at[i]) for i, (a, b) in enumerate(zip(sources, held))]
        for copy in copies:
            copy.start()

        def need(*wanted):
            for i, ref in enumerate(held):
                if i not in need.waited and any(ref is w for w in wanted):
                    need.waited.add(i)
                    copies[i].wait()

        need.waited = set()

        body(need, *refs[: inputs - count], *held, *refs[inputs : len(refs) - count - 1])

    return run


def lazy_call(body, name, out_shapes, args, specs, late, scratch=(), micros=1):
    inputs = len(args) + len(late)
    run = lazy(len(late), body)
    return call(
        lambda *refs: run(inputs, *refs),
        name,
        out_shapes,
        (*args, *late),
        list(specs) + [pl.BlockSpec(memory_space=pl.ANY)] * len(late),
        scratch=list(scratch)
        + [pltpu.VMEM(x.shape, x.dtype) for x in late]
        + [pltpu.SemaphoreType.DMA((len(late),))],
        micros=micros,
        grant=56,
    )


VM = pl.BlockSpec(memory_space=pltpu.VMEM)
SM = pl.BlockSpec(memory_space=pltpu.SMEM)


def element(shape, which):
    return pl.BlockSpec((1,) + tuple(shape[1:]), lambda i: (which,) + (0,) * (len(shape) - 1))


def part(shape, which):
    if len(shape) == 3:
        return VM
    return pl.BlockSpec((shape[0], None) + tuple(shape[2:]), lambda i: (0, which, 0, 0))


class Plan:
    def __init__(self, mesh, pattern, values, obs_block, obs_matrix):
        self.row, self.obs = mesh.shape["row"], mesh.shape["obs"]
        self.tm = mesh.shape["tm"]
        self.n = self.row * self.obs
        self.number, self.per_row = pattern.shape[1:]
        self.panel = values.shape[1]
        self.states = self.panel * self.n
        self.width = self.states // self.number
        self.items = obs_block.shape[1]
        self.share = obs_matrix.shape[1]
        self.swapped = self.n == 8 and self.panel % 128 == 0

    def source(self, info, k):
        return lax.bitwise_xor(info[0], k) if self.swapped else k

    def rows_of(self, info, k):
        start = self.source(info, k) * self.panel
        return pl.ds(pl.multiple_of(start, self.panel) if self.swapped else start, self.panel)


def exchange(x, axes, mask, size):
    return lax.ppermute(x, axes, [(a, a ^ mask) for a in range(size)])


def first_leg(plan, x):
    if plan.swapped:
        return [x] + [exchange(x, PLANE, k, plan.n) for k in (2, 4, 6)]
    return [lax.all_gather(x, PLANE, axis=0)]


def second_leg(plan, pieces):
    if plan.swapped:
        even = jnp.stack(pieces)
        return even, exchange(even, PLANE, 1, plan.n)
    return pieces[0][0::2], pieces[0][1::2]


def other_core(plan, even, odd):
    if plan.swapped:
        return exchange(even, PLANE, 1, plan.n)
    return earlier(plan, odd)


def gather(plan, x):
    return second_leg(plan, first_leg(plan, x))


def tie(*trees):
    return lax.optimization_barrier(trees)


def swap_blocks(plan, x):
    return lax.all_to_all(x, PLANE, 0, 0, tiled=True)


def earlier(plan, x):
    return lax.ppermute(x, "tm", [(i, i - 1) for i in range(1, plan.tm)])


def gain_step(plan, info, blocks, pieces, covariance, offsets, data):
    share, panel, items = plan.share, plan.panel, plan.items

    def body(info, blocks, *refs):
        parts = refs[: plan.obs]
        cov, off, dat, message, obs = refs[plan.obs :]
        for k, part in enumerate(parts):
            start = pl.multiple_of(lax.bitwise_xor(info[1], k) * share, share)
            obs[:, pl.ds(start, share), :] = part[...]
        factor = dense_factor(obs[1], blocks[1:2, :], plan.number)
        message[:panel, :] = mm(cov[0], factor, NT)
        message[panel:, :] = jnp.zeros((SMALL, items), F32)
        message[panel : panel + 2, :panel] = off[...]
        spread = jnp.concatenate([dat[...], jnp.zeros((2, items - share), F32)], axis=1)
        spread = jnp.concatenate([spread, jnp.zeros((6, items), F32)], axis=0)
        message[panel + 2 : panel + 4, :] = pltpu.roll(spread, info[1] * share, 1)[:2]

    return call(
        body,
        "gain",
        [(panel + SMALL, items), (2, items, 2 * plan.width)],
        (info, blocks, *pieces, covariance, offsets, data),
        [SM, VM] + [VM] * plan.obs + [element(covariance.shape, 0), VM, VM],
        grant=56,
        micros=1,
    )


def system_step(plan, info, ints, even, odd, obs):
    states, items, panel = plan.states, plan.items, plan.panel

    def body(info, ints, even, odd, obs, gains, pack):
        tail = items
        zeta = jnp.zeros((2, items), F32)
        end = tail + SMALL * plan.number
        pack[tail:end, :] = jnp.zeros((SMALL * plan.number, items), F32)
        for e in range(2):
            for h in range(2):
                at = end + (2 * e + h) * items
                pack[at : at + items, :] = obs[e, :, h * plan.width : (h + 1) * plan.width]
        for k in range(plan.n):
            piece = (even, odd)[k % 2]
            gains[plan.rows_of(info, k), :] = piece[k // 2, :panel, :]
            start = plan.source(info, k) * panel
            if plan.swapped:
                block = start // plan.width
                at = pl.multiple_of(tail + block * SMALL, SMALL)
                pack[pl.ds(at, 2), :] = piece[k // 2, panel : panel + 2, :]
            else:
                at = tail + start // plan.width * SMALL
                lane = start % plan.width
                pack[at : at + 2, lane : lane + panel] = piece[k // 2, panel : panel + 2, :panel]
            if k < plan.obs:
                zeta = zeta + piece[k // 2, panel + 2 : panel + 4, :]
        pack[tail + 2 : tail + 4, :] = zeta
        factor = dense_factor(obs[1], ints[1:2, :items], plan.number)
        system = identity(items) + mm(factor, gains[...])
        pack[:tail, :] = inverse_factor(system)

    return call(
        body,
        "system",
        [(states, items), (5 * items + SMALL * plan.number, items)],
        (info, ints, even, odd, obs),
        [SM, VM, VM, VM, VM],
        micros=20,
    )


def fill(plan, info, even, odd, out):
    for k in range(plan.n):
        out[plan.rows_of(info, k), :] = (even, odd)[k % 2][k // 2, : plan.panel]


def starts(plan, ints, which, c):
    return [
        pl.multiple_of(ints[which, plan.items + c * plan.per_row + k] * plan.width, plan.width)
        for k in range(plan.per_row)
    ]


def spread_step(plan, info, ints, even, odd, covariance):
    states, panel, width = plan.states, plan.panel, plan.width
    wide = plan.per_row * width

    def body(info, ints, even, odd, cov, out, values, high, low):
        fill(plan, info, even, odd, values)
        high[...], low[...] = split(cov[0])
        for c in range(plan.number):
            taken = tuple(
                jnp.concatenate([r[:, pl.ds(s, width)] for s in starts(plan, ints, 1, c)], axis=1)
                for r in (high, low)
            )
            at = slice(c * width, (c + 1) * width)
            out[at, :] = dot3(split(values[at, :]), taken, NT)

    return call(
        body,
        "spread",
        [(states, panel), (states, wide)],
        (info, ints, even, odd, covariance),
        [SM, SM, VM, VM, element(covariance.shape, 0)],
        scratch=[pltpu.VMEM((panel, states), BF16)] * 2,
        micros=1,
    )


def packed_factor(plan, ints, which, pack):
    at = plan.items + SMALL * plan.number + 2 * which * plan.items
    matrix = jnp.concatenate([pack[at + h * plan.items : at + (h + 1) * plan.items, :] for h in range(2)], axis=1)
    return dense_factor(matrix, ints[which : which + 1, : plan.items], plan.number)


def gathered(plan, ints, which, c, refs):
    begins = starts(plan, ints, which, c)
    return tuple(jnp.concatenate([r[pl.ds(s, plan.width), :] for s in begins], axis=0) for r in refs)


def gathered_columns(plan, ints, which, c, refs):
    begins = starts(plan, ints, which, c)
    return tuple(jnp.concatenate([r[:, pl.ds(s, plan.width)] for s in begins], axis=1) for r in refs)


def block(plan, c):
    return slice(c * plan.width, (c + 1) * plan.width)


def beside(first, second, axis):
    return tuple(jnp.concatenate([x, y], axis=axis) for x, y in zip(first, second))


def negative(pair):
    return tuple(-x for x in pair)


def across(plan, ints, which, left, values, out, rows=None):
    if rows is None:
        rows = range(plan.number)
    width = plan.width
    out[...] = jnp.zeros_like(out)
    for i, c in enumerate(rows):
        product = dot3(left(i, c), split(values(c)), NN)
        for k, s in enumerate(starts(plan, ints, which, c)):
            at = pl.ds(s, width)
            out[:, at] = out[:, at] + product[:, k * width : (k + 1) * width]


def columns_of(pair, at):
    return tuple(x[:, at] for x in pair)


def upper_part(plan, ints, factor, inverse, values, upper, seen):
    pair = split(factor)
    across(plan, ints, 0, lambda i, c: columns_of(pair, block(plan, c)), lambda c: values[block(plan, c), :], seen)
    upper[...] = dot3(inverse, split(seen[...]), NN)


def weigh(plan, ints, values, gains, pack, gain_h, gain_l, weights):
    items = plan.items
    inverse = split(pack[:items, :])
    gain_h[...], gain_l[...] = split(dot3(split(gains), inverse, NT))
    for c in range(plan.number):
        weights[block(plan, c), :] = dot3(
            split(values[block(plan, c), :]), gathered(plan, ints, 1, c, (gain_h, gain_l)), NN
        )


def solve_vectors(plan, pack, factor, small):
    items, number = plan.items, plan.number
    tail = items
    vector = jnp.concatenate(
        [pack[tail + c * SMALL : tail + (c + 1) * SMALL, :] for c in range(number)], axis=1
    )
    zeta = pack[tail : tail + SMALL, :]
    residual = zeta[3:4, :] - mm(vector, factor, NT)[0:1, :]
    solved = mm(jnp.broadcast_to(residual, (SMALL, items)), pack[:tail, :], NT)
    small[0:1, :] = solved[0:1, :]
    small[1:2, :] = zeta[2:3, :]
    small[2:, :] = jnp.zeros((SMALL - 2, items), F32)
    return solved


def earlier_offsets(plan, ints, c, pack):
    tail = plan.items
    begins = [
        pl.multiple_of(tail + ints[1, plan.items + c * plan.per_row + k] * SMALL, SMALL)
        for k in range(plan.per_row)
    ]
    return [pack[pl.ds(s, SMALL), :] for s in begins]


def own_block(plan, info):
    start = info[0] * plan.panel
    return start // plan.width, pl.ds(pl.multiple_of(start, plan.panel), plan.panel)


def panel_dynamics(plan, info, ints, first, second, weights, upper_pair, out):
    width = plan.width
    c, mine = own_block(plan, info)
    left = split(second[mine, :])
    middle = [ints[1, plan.items + c * plan.per_row + k] for k in range(plan.per_row)]
    across(
        plan,
        ints,
        0,
        lambda i, c: columns_of(left, slice(i * width, (i + 1) * width)),
        lambda c: first[pl.ds(pl.multiple_of(c * width, width), width), :],
        out,
        middle,
    )
    out[...] = out[...] - dot3(split(weights[mine, :]), upper_pair, NN)


def level_step(plan, info, ints, even, odd, values, gains, pack):
    states, items = plan.states, plan.items

    def body(info, ints, ints_v, even, odd, values, gains, pack, first, weights, upper, small, *scratch):
        seen, gain_h, gain_l = scratch
        fill(plan, info, even, odd, first)
        factor = packed_factor(plan, ints_v, 1, pack)
        inverse = split(pack[:items, :])
        upper_part(plan, ints, factor, inverse, first, upper, seen)
        weigh(plan, ints, values, gains[...], pack, gain_h, gain_l, weights)
        solve_vectors(plan, pack, factor, small)

    return call(
        body,
        "level",
        [(states, plan.per_row * plan.width), (states, items), (items, states), (SMALL, items)],
        (info, ints, ints, even, odd, values, gains, pack),
        [SM, SM, VM, VM, VM, VM, VM, VM],
        scratch=[pltpu.VMEM((items, states), F32)] + [pltpu.VMEM((states, items), BF16)] * 2,
        grant=56,
        micros=1,
    )


def later_upper_step(plan, info, ints, even, odd, pack):
    states, items = plan.states, plan.items

    def body(info, ints, ints_v, even, odd, pack, first, upper, seen):
        fill(plan, info, even, odd, first)
        factor = packed_factor(plan, ints_v, 1, pack)
        inverse = split(pack[:items, :])
        upper_part(plan, ints, factor, inverse, first, upper, seen)

    return call(
        body,
        "later_upper",
        [(states, plan.per_row * plan.width), (items, states)],
        (info, ints, ints, even, odd, pack),
        [SM, SM, VM, part(even.shape, 0), part(odd.shape, 0), VM],
        scratch=[pltpu.VMEM((items, states), F32)],
        micros=1,
    )


def later_level_step(plan, info, ints, even, odd, gain_even, gain_odd, first, upper, pack, cov):
    states, items, panel = plan.states, plan.items, plan.panel

    def body(info, ints, even, odd, gain_even, gain_odd, first, upper, pack, cov, second, weights, out, *scratch):
        gains, gain_h, gain_l, cov_h, cov_l, part_h, part_l = scratch
        fill(plan, info, even, odd, second)
        fill(plan, info, gain_even, gain_odd, gains)
        weigh(plan, ints, second, gains[...], pack, gain_h, gain_l, weights)
        cov_h[...], cov_l[...] = split(cov[...])
        upper_pair = split(upper[...])
        rest = split(dot3(upper_pair, (cov_h[...], cov_l[...]), NT))
        for c in range(plan.number):
            at = block(plan, c)
            taken = gathered_columns(plan, ints, 0, c, (cov_h, cov_l))
            part_h[at, :], part_l[at, :] = split(dot3(split(first[at, :]), taken, NT))
        for c in range(plan.number):
            at = block(plan, c)
            left = beside(split(second[at, :]), negative(split(weights[at, :])), 1)
            out[at, :] = dot3(left, beside(gathered(plan, ints, 1, c, (part_h, part_l)), rest, 0), NN)

    return call(
        body,
        "later_level",
        [
            (states, plan.per_row * plan.width),
            (states, items),
            (states, panel),
        ],
        (info, ints, even, odd, gain_even, gain_odd, first, upper, pack, cov),
        [SM, SM, part(even.shape, 1), part(odd.shape, 1), VM, VM, VM, VM, VM, VM],
        scratch=[pltpu.VMEM((states, items), F32)]
        + [pltpu.VMEM((states, items), BF16)] * 2
        + [pltpu.VMEM((panel, states), BF16)] * 2
        + [pltpu.VMEM((states, panel), BF16)] * 2,
        grant=56,
        micros=1,
    )


def ahead_step(plan, info, ints, later_ints, first, second, weights, upper, later_first, later_second, later_weights, later_upper, later_pack):
    states, items, panel, width = plan.states, plan.items, plan.panel, plan.width

    def body(
        info, ints, later_ints, ints_v, first, second, weights, upper,
        later_first, later_second, later_weights, later_upper, pack,
        out, dyn, small, offset, column, high, low,
    ):
        c, _ = own_block(plan, info)
        for r in range(plan.number):
            total = jnp.zeros((width, width), F32)
            for k in range(plan.per_row):
                here = ints[0, items + r * plan.per_row + k] == c
                total = total + jnp.where(here, first[block(plan, r), k * width : (k + 1) * width], 0.0)
            if panel % width:
                total = pltpu.roll(total, width - lax.rem(info[0] * panel, width), 1)
            column[block(plan, r), :] = total[:, :panel]
        high[...], low[...] = split(column[...])
        if panel % width:
            shift = states - info[0] * panel
            rest = split(pltpu.roll(upper[...], shift, 1)[:, :panel])
        else:
            rest = split(upper[:, own_block(plan, info)[1]])
        for r in range(plan.number):
            at = block(plan, r)
            left = beside(split(second[at, :]), negative(split(weights[at, :])), 1)
            column[at, :] = dot3(left, beside(gathered(plan, ints, 1, r, (high, low)), rest, 0), NN)
        factor = jnp.concatenate(
            [later_upper[...], packed_factor(plan, ints_v, 0, pack)], axis=0
        )
        out[...] = mm(factor, column[...], NN)
        panel_dynamics(plan, info, later_ints, later_first, later_second, later_weights, split(later_upper[...]), dyn)
        solved = solve_vectors(plan, pack, packed_factor(plan, ints_v, 1, pack), small)
        c, mine = own_block(plan, info)
        left = jnp.concatenate(earlier_offsets(plan, later_ints, c, pack) + [solved], axis=1)
        right = jnp.concatenate([later_second[mine, :], later_weights[mine, :]], axis=1)
        own = pack[pl.ds(pl.multiple_of(items + c * SMALL, SMALL), SMALL), :]
        if panel % width:
            own = pltpu.roll(own, width - lax.rem(info[0] * panel, width), 1)[:, :panel]
        offset[...] = mm(left, right, NT) + jnp.broadcast_to(own[1:2, :], (SMALL, panel))

    return call(
        body,
        "ahead",
        [(2 * items, panel), (panel, states), (SMALL, items), (SMALL, panel)],
        (
            info, ints, later_ints, later_ints, first, second, weights, upper,
            later_first, later_second, later_weights, later_upper, later_pack,
        ),
        [SM, SM, SM] + [VM] * 10,
        scratch=[pltpu.VMEM((states, panel), F32)] + [pltpu.VMEM((states, panel), BF16)] * 2,
        grant=56,
        micros=1,
    )


def covariance_step(plan, info, ints, moved, values, weights, covariance, pack, small):
    states, panel, items = plan.states, plan.panel, plan.items
    tail = items

    def body(info, ints, moved, values, weights, cov, pack, small, out, offset, held_h, held_l):
        for a in range(plan.n):
            at = slice(a * panel, (a + 1) * panel)
            held_h[:, at], held_l[:, at] = split(moved[a])
        mine = own_block(plan, info)[1]
        solved = jnp.broadcast_to(small[0:1, :], (SMALL, items))
        last = split(jnp.concatenate([-weights[mine, :], solved], axis=0))
        for c in range(plan.number):
            at = block(plan, c)
            top = gathered_columns(plan, ints, 1, c, (held_h, held_l))
            low = split(jnp.concatenate(earlier_offsets(plan, ints, c, pack), axis=1))
            left = beside(beside(top, low, 0), last, 1)
            right = beside(split(values[at, :]), split(weights[at, :]), 1)
            result = dot3(left, right, NT)
            out[:, at] = result[:panel, :] + cov[0, :, at]
            own = pack[tail + c * SMALL : tail + (c + 1) * SMALL, :]
            offset[:, at] = result[panel:, :] + jnp.broadcast_to(own[1:2, :], (SMALL, items))

    return call(
        body,
        "covariance",
        [(panel, states), (SMALL, states)],
        (info, ints, moved, values, weights, covariance, pack, small),
        [SM, SM, VM, VM, VM, element(covariance.shape, 1), VM, VM],
        scratch=[pltpu.VMEM((panel, states), BF16)] * 2,
        grant=56,
        micros=1,
    )


def later_gain_step(plan, ints, cov, upper, pack):
    items = plan.items

    def body(ints, cov, upper, pack, out):
        factor = jnp.concatenate([upper[...], packed_factor(plan, ints, 0, pack)], axis=0)
        out[...] = mm(cov[...], factor, NT)

    return call(
        body,
        "later_gain",
        [(plan.panel, 2 * items)],
        (ints, cov, upper, pack),
        [VM, VM, VM, VM],
        micros=1,
    )[0]


def finish_step(plan, info, ints, later_ints, own, later, covs, later_gains, moved, seen, pack, later_pack):
    states, items, panel, number = plan.states, plan.items, plan.panel, plan.number
    rank = 2 * items

    def body(
        need, info, ints, later_ints, ints_v, later_ints_v, own_small, own_offset, later_small, later_offset,
        even, odd, later_upper, later_pack, later_first, later_second, later_weights, moved, later_cov,
        later_dyn, second, first, own_weights, own_upper, pack, seen, own_cov,
        out_dyn, out_off, out_cov, out_fac, out_info,
        gain_h, gain_l, part_h, part_l, held_h, held_l, side_h, side_l, carried, weights, fac, dyn, half,
    ):
        mine = own_block(plan, info)[1]

        def own_columns(ref):
            if panel % 128 == 0:
                return ref[:, mine]
            return pltpu.roll(ref[...], states - info[0] * panel, 1)[:, :panel]

        need(even, odd, later_upper, later_pack, later_first, later_second, later_weights, moved, later_cov)
        for k in range(plan.n):
            at = plan.rows_of(info, k)
            gain_h[at, :], gain_l[at, :] = split((even, odd)[k % 2][k // 2])
        pair = (gain_h[...], gain_l[...])
        factor = jnp.concatenate([later_upper[...], packed_factor(plan, later_ints_v, 0, later_pack)], axis=0)
        factor_pair = split(factor)
        system = dot3(factor_pair, pair, NN)
        above, below = system[:items, :], system[items:, :]
        top = inverse_factor(identity(items) + above[:, :items])
        for c in range(number):
            at = block(plan, c)
            taken = gathered(plan, later_ints, 0, c, (gain_h, gain_l))
            part_h[at, :], part_l[at, :] = split(dot3(split(later_first[at, :]), taken, NN))
        for a in range(plan.n):
            at = slice(a * panel, (a + 1) * panel)
            held_h[:, at], held_l[:, at] = split(moved[a])
        rest = split(above)
        side_rest = negative(split(dot3((held_h[...], held_l[...]), split(later_upper[...]), NT)))
        for c in range(number):
            at = block(plan, c)
            taken = gathered_columns(plan, later_ints, 0, c, (held_h, held_l))
            side_h[:, at], side_l[:, at] = split(dot3(taken, split(later_first[at, :]), NT))
        lower = mm(below[:, :items], top, NT)
        bottom = inverse_factor(identity(items) + below[:, items:] - mm(lower, lower, NT))
        for c in range(number):
            at = block(plan, c)
            own = split(later_second[at, :])
            weight = split(later_weights[at, :])
            carried[at, :] = dot3(
                beside(own, negative(weight), 1), beside(gathered(plan, later_ints, 1, c, (part_h, part_l)), rest, 0), NN
            )
            taken = gathered_columns(plan, later_ints, 1, c, (side_h, side_l))
            half[:, at] = dot3(beside(taken, side_rest, 1), beside(own, weight, 1), NT) + later_cov[:, at]
        corner = -mm(bottom, mm(lower, top))
        inverse = jnp.concatenate(
            [
                jnp.concatenate([top, jnp.zeros((items, items), F32)], axis=1),
                jnp.concatenate([corner, bottom], axis=1),
            ],
            axis=0,
        )
        inverse_pair = split(inverse)
        need(later_dyn, second, first, own_weights, own_upper, pack, seen, own_cov)
        fac[...] = packed_factor(plan, ints_v, 0, pack)
        last = [jnp.transpose(own_columns(own_upper)), jnp.transpose(own_columns(fac))]

        @pl.when(info[2] == 0)
        def _():
            panel_dynamics(plan, info, ints, first, second, own_weights, split(own_upper[...]), dyn)
            out_dyn[0] = dyn[...]
            out_off[0] = own_columns(own_offset)[0:1, :]
            out_cov[0] = own_cov[...]
            out_fac[0, :, :items] = last[0]
            out_fac[0, :, items:rank] = last[1]
            out_fac[0, :, rank:] = jnp.zeros((panel, rank), F32)
            zeta = jnp.concatenate([own_small[0:1, :], own_small[1:2, :]], axis=1)
            zeta = jnp.broadcast_to(zeta, (SMALL, rank))
            out_info[0] = mm(zeta, out_fac[0, :, :rank], NT)[0:1, :]

        @pl.when(info[2] == 1)
        def _():
            weights[...] = dot3(split(carried[...]), inverse_pair, NT)
            own_weight = weights[mine, :]
            weight_pair = split(-own_weight)
            left = later_dyn[...] + dot3(split(dot3(weight_pair, inverse_pair, NN)), factor_pair, NN)
            left_pair = split(left)
            out_cov[0] = half[...] + dot3(weight_pair, split(weights[...]), NT)
            across(
                plan, ints, 1, lambda i, c: columns_of(left_pair, block(plan, c)),
                lambda c: second[block(plan, c), :], half,
            )
            middle = split(half[...])
            across(
                plan, ints, 0, lambda i, c: columns_of(middle, block(plan, c)),
                lambda c: first[block(plan, c), :], dyn,
            )
            through = split(dot3(left_pair, split(own_weights[...]), NN))
            out_dyn[0] = dyn[...] - dot3(through, split(own_upper[...]), NN)
            residual = jnp.concatenate([later_small[0:1, :], later_small[1:2, :]], axis=1)
            offset = own_offset[...]
            residual = jnp.broadcast_to(residual, (SMALL, rank)) - dot3(split(offset), factor_pair, NT)
            solved = dot3(split(residual), inverse_pair, NT)
            gone = mm(offset, later_dyn[...], NT) + mm(solved, own_weight, NT)
            out_off[0] = gone[0:1, :] + later_offset[0:1, :]
            out_fac[0, :, :rank] = jnp.transpose(dot3(inverse_pair, split(seen[...]), NN))
            out_fac[0, :, rank : rank + items] = last[0]
            out_fac[0, :, rank + items :] = last[1]
            zeta = jnp.concatenate([solved[0:1, :], own_small[0:1, :], own_small[1:2, :]], axis=1)
            zeta = jnp.broadcast_to(zeta, (SMALL, 2 * rank))
            out_info[0] = mm(zeta, out_fac[0], NT)[0:1, :]

    even, odd = later_gains
    first, second, own_weights, own_upper, own_small, own_offset = own
    later_first, later_second, later_weights, later_upper, later_small, later_dyn, later_offset = later
    own_cov, later_cov = covs
    return lazy_call(
        body,
        "finish",
        [
            (1, panel, states),
            (1, 1, panel),
            (1, panel, states),
            (1, panel, 2 * rank),
            (1, 1, panel),
        ],
        (info, ints, later_ints, ints, later_ints, own_small, own_offset, later_small, later_offset),
        [SM] * 3 + [VM] * 6,
        (
            even, odd, later_upper, later_pack, later_first, later_second, later_weights, moved, later_cov,
            later_dyn, second, first, own_weights, own_upper, pack, seen, own_cov,
        ),
        scratch=[pltpu.VMEM((states, rank), BF16)] * 4
        + [pltpu.VMEM((panel, states), BF16)] * 4
        + [pltpu.VMEM((states, rank), F32)] * 2
        + [pltpu.VMEM((items, states), F32)]
        + [pltpu.VMEM((panel, states), F32)] * 2,
        micros=20,
    )


def per_device(mesh, dyn_pattern, dyn_values, offsets, covariance, obs_block, obs_matrix, obs_data):
    plan = Plan(mesh, dyn_pattern, dyn_values, obs_block, obs_matrix)
    here = lax.axis_index(PLANE)
    even_turn = 1 - lax.axis_index("tm") % 2
    info = jnp.stack([here, lax.axis_index("obs"), even_turn]).astype(jnp.int32)
    ints = jnp.concatenate([obs_block, dyn_pattern.reshape(2, -1)], axis=1)

    pieces = [obs_matrix] + [exchange(obs_matrix, "obs", k, plan.obs) for k in range(1, plan.obs)]
    later_ints = earlier(plan, ints)
    own_first, own_second = dyn_values[0], dyn_values[1]
    pieces, own_first, own_second = tie(pieces, own_first, own_second)
    later_values = earlier(plan, own_first)
    message, obs = gain_step(plan, info, obs_block, pieces, covariance, offsets, obs_data)
    gain_leg_one = first_leg(plan, message)
    gain_leg_one, own_second, own_first, later_ints = tie(gain_leg_one, own_second, own_first, later_ints)
    gain_even, gain_odd = second_leg(plan, gain_leg_one)
    later_gain_even = earlier(plan, gain_even)
    second_leg_one = first_leg(plan, own_second)
    gains, pack = system_step(plan, info, ints, gain_even, gain_odd, obs)
    pack, second_leg_one, own_first, later_values, later_gain_even = tie(
        pack, second_leg_one, own_first, later_values, later_gain_even
    )
    later_pack = earlier(plan, pack)
    second_even, second_odd = second_leg(plan, second_leg_one)
    later_second_even = earlier(plan, second_even)
    first_leg_one = first_leg(plan, own_first)

    spread, second = spread_step(plan, info, ints, second_even, second_odd, covariance)
    first_leg_one, second, later_values, later_pack, later_gain_even = tie(
        first_leg_one, second, later_values, later_pack, later_gain_even
    )
    moved = swap_blocks(plan, spread.reshape(plan.n, plan.panel, plan.panel))
    first_even, first_odd = second_leg(plan, first_leg_one)
    later_leg_one = first_leg(plan, later_values)
    later_gain_odd = other_core(plan, later_gain_even, gain_odd)
    first, weights, upper, small = level_step(plan, info, ints, first_even, first_odd, second, gains, pack)
    moved, weights, later_leg_one = tie(moved, weights, later_leg_one)
    later_even, later_odd = second_leg(plan, later_leg_one)
    cov, offset = covariance_step(plan, info, ints, moved, second, weights, covariance, pack, small)
    later_second_even, offset = tie(later_second_even, offset)
    later_second_odd = other_core(plan, later_second_even, second_odd)
    own = (first, second, weights, upper, small, offset)
    later_cov = earlier(plan, cov)

    later_first, later_upper = later_upper_step(plan, info, later_ints, later_even, later_odd, later_pack)
    gain = later_gain_step(plan, later_ints, cov, later_upper, later_pack)
    gain_leg_one = first_leg(plan, gain)
    later_second, later_weights, spread = later_level_step(
        plan, info, later_ints, later_second_even, later_second_odd, later_gain_even, later_gain_odd,
        later_first, later_upper, later_pack, cov,
    )
    moved = swap_blocks(plan, spread.reshape(plan.n, plan.panel, plan.panel))
    gain_leg_one, later_weights = tie(gain_leg_one, later_weights)
    gain_even, gain_odd = second_leg(plan, gain_leg_one)
    seen, later_dyn, later_small, later_offset = ahead_step(
        plan, info, ints, later_ints, first, second, weights, upper,
        later_first, later_second, later_weights, later_upper, later_pack,
    )
    later = (later_first, later_second, later_weights, later_upper, later_small, later_dyn, later_offset)
    dyn, off, cov, fac, information = finish_step(
        plan, info, ints, later_ints, own, later, (cov, later_cov), (gain_even, gain_odd), moved, seen, pack, later_pack
    )
    return dyn, off[:, 0], cov, fac, information[:, 0]


def solution(mesh):
    placed = (
        P("tm", None, None),
        P("tm", PLANE, None),
        P("tm", PLANE),
        P("tm", PLANE, None),
        P("tm", None),
        P("tm", "obs", None),
        P("tm", "obs"),
    )

    def run(*arrays):
        return per_device(mesh, *arrays)

    return jax.shard_map(
        run,
        mesh=mesh,
        in_specs=placed,
        out_specs=(
            P("tm", PLANE, None),
            P("tm", PLANE),
            P("tm", PLANE, None),
            P("tm", PLANE, None),
            P("tm", PLANE),
        ),
        check_vma=False,
    )
```

```python
import jax
import jax.numpy as jnp
from jax import lax
from jax.experimental import pallas as pl
from jax.experimental.pallas import tpu as pltpu
from jax.sharding import PartitionSpec as P

F32 = jnp.float32
BF16 = jnp.bfloat16
NN = (((1,), (0,)), ((), ()))
NT = (((1,), (1,)), ((), ()))
PLANE = ("row", "obs")
SMALL = 8


def split(x):
    high = x.astype(BF16)
    return high, (x - high.astype(F32)).astype(BF16)


def dot3(left, right, dims):
    (a, b), (c, d) = left, right
    return lax.dot_general(
        jnp.concatenate([a, a, b], axis=1),
        jnp.concatenate([c, d, c], axis=dims[0][1][0]),
        dims,
        preferred_element_type=F32,
    )


def mm(left, right, dims=NN):
    return dot3(split(left), split(right), dims)


def reciprocal(x):
    y = pl.reciprocal(x, approx=True)
    return y * (2.0 - x * y)


def inverse_root(x):
    y = lax.rsqrt(x)
    return y * (1.5 - (0.5 * x) * (y * y))


def inverse_factor(matrix):
    size = matrix.shape[0]
    tiles = size // 8
    sub = lax.broadcasted_iota(jnp.int32, (8, size), 0)
    lane = lax.broadcasted_iota(jnp.int32, (8, size), 1)

    def wide(x):
        return jnp.broadcast_to(x, (8, size))

    rows = [matrix[8 * t : 8 * t + 8, :] for t in range(tiles)]
    inverse = [jnp.where(lane == sub + 8 * t, 1.0, 0.0).astype(F32) for t in range(tiles)]
    for p in range(tiles):
        column = {
            (t, c): wide(rows[t][:, 8 * p + c : 8 * p + c + 1])
            for t in range(p, tiles)
            for c in range(8)
        }
        scale = None
        for r in range(8):
            pivot = wide(column[p, r][r : r + 1, :])
            over = reciprocal(pivot)
            root = inverse_root(pivot)
            scale = root if r == 0 else jnp.where(sub == r, root, scale)
            factor = {t: column[t, r] * over for t in range(p, tiles)}
            for c in range(r + 1, 8):
                other = wide(column[p, r][c : c + 1, :])
                for t in range(p, tiles):
                    column[t, c] = column[t, c] - factor[t] * other
            factor[p] = jnp.where(sub > r, factor[p], 0.0)
            row_here = wide(rows[p][r : r + 1, :])
            inverse_here = wide(inverse[p][r : r + 1, :])
            for t in range(p, tiles):
                rows[t] = rows[t] - factor[t] * row_here
                inverse[t] = inverse[t] - factor[t] * inverse_here
        inverse[p] = inverse[p] * scale
    return jnp.concatenate(inverse, axis=0)


def identity(size):
    sub = lax.broadcasted_iota(jnp.int32, (size, size), 0)
    lane = lax.broadcasted_iota(jnp.int32, (size, size), 1)
    return jnp.where(sub == lane, 1.0, 0.0).astype(F32)


def dense_factor(matrix, blocks, number):
    items, width = matrix.shape[0], matrix.shape[1] // 2
    at = jnp.transpose(jnp.broadcast_to(blocks.astype(F32), (width, items)))
    pieces = []
    for r in range(number):
        first = jnp.where(at == float(r), matrix[:, :width], 0.0)
        second = jnp.where(at == float((r - 1) % number), matrix[:, width:], 0.0)
        pieces.append(first + second)
    return jnp.concatenate(pieces, axis=1)


def call(body, name, out_shapes, args, specs, scratch=(), micros=1, grant=24):
    return pl.pallas_call(
        body,
        name=name,
        grid=(1,),
        in_specs=specs,
        out_specs=[VM] * len(out_shapes),
        out_shape=[s if isinstance(s, jax.ShapeDtypeStruct) else jax.ShapeDtypeStruct(s, F32) for s in out_shapes],
        scratch_shapes=list(scratch),
        compiler_params=pltpu.CompilerParams(vmem_limit_bytes=grant * 2**20),
        cost_estimate=pl.CostEstimate(flops=micros * 10**9, bytes_accessed=2**20, transcendentals=0),
    )(*args)


def lazy(count, body):
    def run(inputs, *refs):
        sources = refs[inputs - count : inputs]
        held = refs[len(refs) - count - 1 : len(refs) - 1]
        sems = refs[-1]
        copies = [pltpu.make_async_copy(a, b, sems.at[i]) for i, (a, b) in enumerate(zip(sources, held))]
        for copy in copies:
            copy.start()

        def need(*wanted):
            for i, ref in enumerate(held):
                if i not in need.waited and any(ref is w for w in wanted):
                    need.waited.add(i)
                    copies[i].wait()

        need.waited = set()

        body(need, *refs[: inputs - count], *held, *refs[inputs : len(refs) - count - 1])

    return run


def lazy_call(body, name, out_shapes, args, specs, late, scratch=(), micros=1):
    inputs = len(args) + len(late)
    run = lazy(len(late), body)
    return call(
        lambda *refs: run(inputs, *refs),
        name,
        out_shapes,
        (*args, *late),
        list(specs) + [pl.BlockSpec(memory_space=pl.ANY)] * len(late),
        scratch=list(scratch)
        + [pltpu.VMEM(x.shape, x.dtype) for x in late]
        + [pltpu.SemaphoreType.DMA((len(late),))],
        micros=micros,
        grant=56,
    )


VM = pl.BlockSpec(memory_space=pltpu.VMEM)
SM = pl.BlockSpec(memory_space=pltpu.SMEM)


def element(shape, which):
    return pl.BlockSpec((1,) + tuple(shape[1:]), lambda i: (which,) + (0,) * (len(shape) - 1))


def part(shape, which):
    if len(shape) == 3:
        return VM
    return pl.BlockSpec((shape[0], None) + tuple(shape[2:]), lambda i: (0, which, 0, 0))


class Plan:
    def __init__(self, mesh, pattern, values, obs_block, obs_matrix):
        self.row, self.obs = mesh.shape["row"], mesh.shape["obs"]
        self.tm = mesh.shape["tm"]
        self.n = self.row * self.obs
        self.number, self.per_row = pattern.shape[1:]
        self.panel = values.shape[1]
        self.states = self.panel * self.n
        self.width = self.states // self.number
        self.items = obs_block.shape[1]
        self.share = obs_matrix.shape[1]
        self.swapped = self.n == 8 and self.panel % 128 == 0

    def source(self, info, k):
        return lax.bitwise_xor(info[0], k) if self.swapped else k

    def rows_of(self, info, k):
        start = self.source(info, k) * self.panel
        return pl.ds(pl.multiple_of(start, self.panel) if self.swapped else start, self.panel)


def exchange(x, axes, mask, size):
    return lax.ppermute(x, axes, [(a, a ^ mask) for a in range(size)])


def first_leg(plan, x):
    if plan.swapped:
        return [x] + [exchange(x, PLANE, k, plan.n) for k in (2, 4, 6)]
    return [lax.all_gather(x, PLANE, axis=0)]


def second_leg(plan, pieces):
    if plan.swapped:
        even = jnp.stack(pieces)
        return even, exchange(even, PLANE, 1, plan.n)
    return pieces[0][0::2], pieces[0][1::2]


def other_core(plan, even, odd):
    if plan.swapped:
        return exchange(even, PLANE, 1, plan.n)
    return earlier(plan, odd)


def gather(plan, x):
    return second_leg(plan, first_leg(plan, x))


def tie(*trees):
    return lax.optimization_barrier(trees)


def swap_blocks(plan, x):
    return lax.all_to_all(x, PLANE, 0, 0, tiled=True)


def earlier(plan, x):
    return lax.ppermute(x, "tm", [(i, i - 1) for i in range(1, plan.tm)])


def gain_step(plan, info, blocks, pieces, covariance, offsets, data):
    share, panel, items = plan.share, plan.panel, plan.items

    def body(info, blocks, *refs):
        parts = refs[: plan.obs]
        cov, off, dat, message, obs = refs[plan.obs :]
        for k, part in enumerate(parts):
            start = pl.multiple_of(lax.bitwise_xor(info[1], k) * share, share)
            obs[:, pl.ds(start, share), :] = part[...]
        factor = dense_factor(obs[1], blocks[1:2, :], plan.number)
        message[:panel, :] = mm(cov[0], factor, NT)
        message[panel:, :] = jnp.zeros((SMALL, items), F32)
        message[panel : panel + 2, :panel] = off[...]
        spread = jnp.concatenate([dat[...], jnp.zeros((2, items - share), F32)], axis=1)
        spread = jnp.concatenate([spread, jnp.zeros((6, items), F32)], axis=0)
        message[panel + 2 : panel + 4, :] = pltpu.roll(spread, info[1] * share, 1)[:2]

    return call(
        body,
        "gain",
        [(panel + SMALL, items), (2, items, 2 * plan.width)],
        (info, blocks, *pieces, covariance, offsets, data),
        [SM, VM] + [VM] * plan.obs + [element(covariance.shape, 0), VM, VM],
        grant=56,
        micros=1,
    )


def system_step(plan, info, ints, even, odd, obs):
    states, items, panel = plan.states, plan.items, plan.panel

    def body(info, ints, even, odd, obs, gains, pack):
        tail = items
        zeta = jnp.zeros((2, items), F32)
        end = tail + SMALL * plan.number
        pack[tail:end, :] = jnp.zeros((SMALL * plan.number, items), F32)
        for e in range(2):
            for h in range(2):
                at = end + (2 * e + h) * items
                pack[at : at + items, :] = obs[e, :, h * plan.width : (h + 1) * plan.width]
        for k in range(plan.n):
            piece = (even, odd)[k % 2]
            gains[plan.rows_of(info, k), :] = piece[k // 2, :panel, :]
            start = plan.source(info, k) * panel
            if plan.swapped:
                block = start // plan.width
                at = pl.multiple_of(tail + block * SMALL, SMALL)
                pack[pl.ds(at, 2), :] = piece[k // 2, panel : panel + 2, :]
            else:
                at = tail + start // plan.width * SMALL
                lane = start % plan.width
                pack[at : at + 2, lane : lane + panel] = piece[k // 2, panel : panel + 2, :panel]
            if k < plan.obs:
                zeta = zeta + piece[k // 2, panel + 2 : panel + 4, :]
        pack[tail + 2 : tail + 4, :] = zeta
        factor = dense_factor(obs[1], ints[1:2, :items], plan.number)
        system = identity(items) + mm(factor, gains[...])
        pack[:tail, :] = inverse_factor(system)

    return call(
        body,
        "system",
        [(states, items), (5 * items + SMALL * plan.number, items)],
        (info, ints, even, odd, obs),
        [SM, VM, VM, VM, VM],
        micros=20,
    )


def fill(plan, info, even, odd, out):
    for k in range(plan.n):
        out[plan.rows_of(info, k), :] = (even, odd)[k % 2][k // 2, : plan.panel]


def starts(plan, ints, which, c):
    return [
        pl.multiple_of(ints[which, plan.items + c * plan.per_row + k] * plan.width, plan.width)
        for k in range(plan.per_row)
    ]


def spread_step(plan, info, ints, even, odd, covariance):
    states, panel, width = plan.states, plan.panel, plan.width
    wide = plan.per_row * width

    def body(info, ints, even, odd, cov, out, values, high, low):
        fill(plan, info, even, odd, values)
        high[...], low[...] = split(cov[0])
        for c in range(plan.number):
            taken = tuple(
                jnp.concatenate([r[:, pl.ds(s, width)] for s in starts(plan, ints, 1, c)], axis=1)
                for r in (high, low)
            )
            at = slice(c * width, (c + 1) * width)
            out[at, :] = dot3(split(values[at, :]), taken, NT)

    return call(
        body,
        "spread",
        [(states, panel), (states, wide)],
        (info, ints, even, odd, covariance),
        [SM, SM, VM, VM, element(covariance.shape, 0)],
        scratch=[pltpu.VMEM((panel, states), BF16)] * 2,
        micros=1,
    )


def packed_factor(plan, ints, which, pack):
    at = plan.items + SMALL * plan.number + 2 * which * plan.items
    matrix = jnp.concatenate([pack[at + h * plan.items : at + (h + 1) * plan.items, :] for h in range(2)], axis=1)
    return dense_factor(matrix, ints[which : which + 1, : plan.items], plan.number)


def gathered(plan, ints, which, c, refs):
    begins = starts(plan, ints, which, c)
    return tuple(jnp.concatenate([r[pl.ds(s, plan.width), :] for s in begins], axis=0) for r in refs)


def gathered_columns(plan, ints, which, c, refs):
    begins = starts(plan, ints, which, c)
    return tuple(jnp.concatenate([r[:, pl.ds(s, plan.width)] for s in begins], axis=1) for r in refs)


def block(plan, c):
    return slice(c * plan.width, (c + 1) * plan.width)


def beside(first, second, axis):
    return tuple(jnp.concatenate([x, y], axis=axis) for x, y in zip(first, second))


def negative(pair):
    return tuple(-x for x in pair)


def across(plan, ints, which, left, values, out, rows=None):
    if rows is None:
        rows = range(plan.number)
    width = plan.width
    out[...] = jnp.zeros_like(out)
    for i, c in enumerate(rows):
        product = dot3(left(i, c), split(values(c)), NN)
        for k, s in enumerate(starts(plan, ints, which, c)):
            at = pl.ds(s, width)
            out[:, at] = out[:, at] + product[:, k * width : (k + 1) * width]


def columns_of(pair, at):
    return tuple(x[:, at] for x in pair)


def upper_part(plan, ints, factor, inverse, values, upper, seen):
    pair = split(factor)
    across(plan, ints, 0, lambda i, c: columns_of(pair, block(plan, c)), lambda c: values[block(plan, c), :], seen)
    upper[...] = dot3(inverse, split(seen[...]), NN)


def weigh(plan, ints, values, gains, pack, gain_h, gain_l, weights):
    items = plan.items
    inverse = split(pack[:items, :])
    gain_h[...], gain_l[...] = split(dot3(split(gains), inverse, NT))
    for c in range(plan.number):
        weights[block(plan, c), :] = dot3(
            split(values[block(plan, c), :]), gathered(plan, ints, 1, c, (gain_h, gain_l)), NN
        )


def solve_vectors(plan, pack, factor, small):
    items, number = plan.items, plan.number
    tail = items
    vector = jnp.concatenate(
        [pack[tail + c * SMALL : tail + (c + 1) * SMALL, :] for c in range(number)], axis=1
    )
    zeta = pack[tail : tail + SMALL, :]
    residual = zeta[3:4, :] - mm(vector, factor, NT)[0:1, :]
    solved = mm(jnp.broadcast_to(residual, (SMALL, items)), pack[:tail, :], NT)
    small[0:1, :] = solved[0:1, :]
    small[1:2, :] = zeta[2:3, :]
    small[2:, :] = jnp.zeros((SMALL - 2, items), F32)
    return solved


def earlier_offsets(plan, ints, c, pack):
    tail = plan.items
    begins = [
        pl.multiple_of(tail + ints[1, plan.items + c * plan.per_row + k] * SMALL, SMALL)
        for k in range(plan.per_row)
    ]
    return [pack[pl.ds(s, SMALL), :] for s in begins]


def own_block(plan, info):
    start = info[0] * plan.panel
    return start // plan.width, pl.ds(pl.multiple_of(start, plan.panel), plan.panel)


def panel_dynamics(plan, info, ints, first, second, weights, upper_pair, out):
    width = plan.width
    c, mine = own_block(plan, info)
    left = split(second[mine, :])
    middle = [ints[1, plan.items + c * plan.per_row + k] for k in range(plan.per_row)]
    across(
        plan,
        ints,
        0,
        lambda i, c: columns_of(left, slice(i * width, (i + 1) * width)),
        lambda c: first[pl.ds(pl.multiple_of(c * width, width), width), :],
        out,
        middle,
    )
    out[...] = out[...] - dot3(split(weights[mine, :]), upper_pair, NN)


def level_step(plan, info, ints, even, odd, values, gains, pack):
    states, items = plan.states, plan.items

    def body(info, ints, ints_v, even, odd, values, gains, pack, first, weights, upper, small, *scratch):
        seen, gain_h, gain_l = scratch
        fill(plan, info, even, odd, first)
        factor = packed_factor(plan, ints_v, 1, pack)
        inverse = split(pack[:items, :])
        upper_part(plan, ints, factor, inverse, first, upper, seen)
        weigh(plan, ints, values, gains[...], pack, gain_h, gain_l, weights)
        solve_vectors(plan, pack, factor, small)

    return call(
        body,
        "level",
        [(states, plan.per_row * plan.width), (states, items), (items, states), (SMALL, items)],
        (info, ints, ints, even, odd, values, gains, pack),
        [SM, SM, VM, VM, VM, VM, VM, VM],
        scratch=[pltpu.VMEM((items, states), F32)] + [pltpu.VMEM((states, items), BF16)] * 2,
        grant=56,
        micros=1,
    )


def later_upper_step(plan, info, ints, even, odd, pack):
    states, items = plan.states, plan.items

    def body(info, ints, ints_v, even, odd, pack, first, upper, seen):
        fill(plan, info, even, odd, first)
        factor = packed_factor(plan, ints_v, 1, pack)
        inverse = split(pack[:items, :])
        upper_part(plan, ints, factor, inverse, first, upper, seen)

    return call(
        body,
        "later_upper",
        [(states, plan.per_row * plan.width), (items, states)],
        (info, ints, ints, even, odd, pack),
        [SM, SM, VM, part(even.shape, 0), part(odd.shape, 0), VM],
        scratch=[pltpu.VMEM((items, states), F32)],
        micros=1,
    )


def later_level_step(plan, info, ints, even, odd, gain_even, gain_odd, first, upper, pack, cov):
    states, items, panel = plan.states, plan.items, plan.panel

    def body(info, ints, even, odd, gain_even, gain_odd, first, upper, pack, cov, second, weights, out, *scratch):
        gains, gain_h, gain_l, cov_h, cov_l, part_h, part_l = scratch
        fill(plan, info, even, odd, second)
        fill(plan, info, gain_even, gain_odd, gains)
        weigh(plan, ints, second, gains[...], pack, gain_h, gain_l, weights)
        cov_h[...], cov_l[...] = split(cov[...])
        upper_pair = split(upper[...])
        rest = split(dot3(upper_pair, (cov_h[...], cov_l[...]), NT))
        for c in range(plan.number):
            at = block(plan, c)
            taken = gathered_columns(plan, ints, 0, c, (cov_h, cov_l))
            part_h[at, :], part_l[at, :] = split(dot3(split(first[at, :]), taken, NT))
        for c in range(plan.number):
            at = block(plan, c)
            left = beside(split(second[at, :]), negative(split(weights[at, :])), 1)
            out[at, :] = dot3(left, beside(gathered(plan, ints, 1, c, (part_h, part_l)), rest, 0), NN)

    return call(
        body,
        "later_level",
        [
            (states, plan.per_row * plan.width),
            (states, items),
            (states, panel),
        ],
        (info, ints, even, odd, gain_even, gain_odd, first, upper, pack, cov),
        [SM, SM, part(even.shape, 1), part(odd.shape, 1), VM, VM, VM, VM, VM, VM],
        scratch=[pltpu.VMEM((states, items), F32)]
        + [pltpu.VMEM((states, items), BF16)] * 2
        + [pltpu.VMEM((panel, states), BF16)] * 2
        + [pltpu.VMEM((states, panel), BF16)] * 2,
        grant=56,
        micros=1,
    )


def ahead_step(plan, info, ints, later_ints, first, second, weights, upper, later_first, later_second, later_weights, later_upper, later_pack):
    states, items, panel, width = plan.states, plan.items, plan.panel, plan.width

    def body(
        info, ints, later_ints, ints_v, first, second, weights, upper,
        later_first, later_second, later_weights, later_upper, pack,
        out, dyn, small, offset, column, high, low,
    ):
        c, _ = own_block(plan, info)
        for r in range(plan.number):
            total = jnp.zeros((width, width), F32)
            for k in range(plan.per_row):
                here = ints[0, items + r * plan.per_row + k] == c
                total = total + jnp.where(here, first[block(plan, r), k * width : (k + 1) * width], 0.0)
            if panel % width:
                total = pltpu.roll(total, width - lax.rem(info[0] * panel, width), 1)
            column[block(plan, r), :] = total[:, :panel]
        high[...], low[...] = split(column[...])
        if panel % width:
            shift = states - info[0] * panel
            rest = split(pltpu.roll(upper[...], shift, 1)[:, :panel])
        else:
            rest = split(upper[:, own_block(plan, info)[1]])
        for r in range(plan.number):
            at = block(plan, r)
            left = beside(split(second[at, :]), negative(split(weights[at, :])), 1)
            column[at, :] = dot3(left, beside(gathered(plan, ints, 1, r, (high, low)), rest, 0), NN)
        factor = jnp.concatenate(
            [later_upper[...], packed_factor(plan, ints_v, 0, pack)], axis=0
        )
        out[...] = mm(factor, column[...], NN)
        panel_dynamics(plan, info, later_ints, later_first, later_second, later_weights, split(later_upper[...]), dyn)
        solved = solve_vectors(plan, pack, packed_factor(plan, ints_v, 1, pack), small)
        c, mine = own_block(plan, info)
        left = jnp.concatenate(earlier_offsets(plan, later_ints, c, pack) + [solved], axis=1)
        right = jnp.concatenate([later_second[mine, :], later_weights[mine, :]], axis=1)
        own = pack[pl.ds(pl.multiple_of(items + c * SMALL, SMALL), SMALL), :]
        if panel % width:
            own = pltpu.roll(own, width - lax.rem(info[0] * panel, width), 1)[:, :panel]
        offset[...] = mm(left, right, NT) + jnp.broadcast_to(own[1:2, :], (SMALL, panel))

    return call(
        body,
        "ahead",
        [(2 * items, panel), (panel, states), (SMALL, items), (SMALL, panel)],
        (
            info, ints, later_ints, later_ints, first, second, weights, upper,
            later_first, later_second, later_weights, later_upper, later_pack,
        ),
        [SM, SM, SM] + [VM] * 10,
        scratch=[pltpu.VMEM((states, panel), F32)] + [pltpu.VMEM((states, panel), BF16)] * 2,
        grant=56,
        micros=1,
    )


def covariance_step(plan, info, ints, moved, values, weights, covariance, pack, small):
    states, panel, items = plan.states, plan.panel, plan.items
    tail = items

    def body(info, ints, moved, values, weights, cov, pack, small, out, offset, held_h, held_l):
        for a in range(plan.n):
            at = slice(a * panel, (a + 1) * panel)
            held_h[:, at], held_l[:, at] = split(moved[a])
        mine = own_block(plan, info)[1]
        solved = jnp.broadcast_to(small[0:1, :], (SMALL, items))
        last = split(jnp.concatenate([-weights[mine, :], solved], axis=0))
        for c in range(plan.number):
            at = block(plan, c)
            top = gathered_columns(plan, ints, 1, c, (held_h, held_l))
            low = split(jnp.concatenate(earlier_offsets(plan, ints, c, pack), axis=1))
            left = beside(beside(top, low, 0), last, 1)
            right = beside(split(values[at, :]), split(weights[at, :]), 1)
            result = dot3(left, right, NT)
            out[:, at] = result[:panel, :] + cov[0, :, at]
            own = pack[tail + c * SMALL : tail + (c + 1) * SMALL, :]
            offset[:, at] = result[panel:, :] + jnp.broadcast_to(own[1:2, :], (SMALL, items))

    return call(
        body,
        "covariance",
        [(panel, states), (SMALL, states)],
        (info, ints, moved, values, weights, covariance, pack, small),
        [SM, SM, VM, VM, VM, element(covariance.shape, 1), VM, VM],
        scratch=[pltpu.VMEM((panel, states), BF16)] * 2,
        grant=56,
        micros=1,
    )


def later_gain_step(plan, ints, cov, upper, pack):
    items = plan.items

    def body(ints, cov, upper, pack, out):
        factor = jnp.concatenate([upper[...], packed_factor(plan, ints, 0, pack)], axis=0)
        out[...] = mm(cov[...], factor, NT)

    return call(
        body,
        "later_gain",
        [(plan.panel, 2 * items)],
        (ints, cov, upper, pack),
        [VM, VM, VM, VM],
        micros=1,
    )[0]


def finish_step(plan, info, ints, later_ints, own, later, covs, later_gains, moved, seen, pack, later_pack):
    states, items, panel, number = plan.states, plan.items, plan.panel, plan.number
    rank = 2 * items

    def body(
        need, info, ints, later_ints, ints_v, later_ints_v, own_small, own_offset, later_small, later_offset,
        even, odd, later_upper, later_pack, later_first, later_second, later_weights, moved, later_cov,
        later_dyn, second, first, own_weights, own_upper, pack, seen, own_cov,
        out_dyn, out_off, out_cov, out_fac, out_info,
        gain_h, gain_l, part_h, part_l, held_h, held_l, side_h, side_l, carried, weights, fac, dyn, half,
    ):
        mine = own_block(plan, info)[1]

        def own_columns(ref):
            if panel % 128 == 0:
                return ref[:, mine]
            return pltpu.roll(ref[...], states - info[0] * panel, 1)[:, :panel]

        need(even, odd, later_upper, later_pack)
        for k in range(plan.n):
            at = plan.rows_of(info, k)
            gain_h[at, :], gain_l[at, :] = split((even, odd)[k % 2][k // 2])
        pair = (gain_h[...], gain_l[...])
        factor = jnp.concatenate([later_upper[...], packed_factor(plan, later_ints_v, 0, later_pack)], axis=0)
        factor_pair = split(factor)
        system = dot3(factor_pair, pair, NN)
        above, below = system[:items, :], system[items:, :]
        need(later_first, later_second, later_weights, moved, later_cov)
        top = inverse_factor(identity(items) + above[:, :items])
        for c in range(number):
            at = block(plan, c)
            taken = gathered(plan, later_ints, 0, c, (gain_h, gain_l))
            part_h[at, :], part_l[at, :] = split(dot3(split(later_first[at, :]), taken, NN))
        for a in range(plan.n):
            at = slice(a * panel, (a + 1) * panel)
            held_h[:, at], held_l[:, at] = split(moved[a])
        rest = split(above)
        side_rest = negative(split(dot3((held_h[...], held_l[...]), split(later_upper[...]), NT)))
        for c in range(number):
            at = block(plan, c)
            taken = gathered_columns(plan, later_ints, 0, c, (held_h, held_l))
            side_h[:, at], side_l[:, at] = split(dot3(taken, split(later_first[at, :]), NT))
        lower = mm(below[:, :items], top, NT)
        bottom = inverse_factor(identity(items) + below[:, items:] - mm(lower, lower, NT))
        for c in range(number):
            at = block(plan, c)
            own = split(later_second[at, :])
            weight = split(later_weights[at, :])
            carried[at, :] = dot3(
                beside(own, negative(weight), 1), beside(gathered(plan, later_ints, 1, c, (part_h, part_l)), rest, 0), NN
            )
            taken = gathered_columns(plan, later_ints, 1, c, (side_h, side_l))
            half[:, at] = dot3(beside(taken, side_rest, 1), beside(own, weight, 1), NT) + later_cov[:, at]
        corner = -mm(bottom, mm(lower, top))
        inverse = jnp.concatenate(
            [
                jnp.concatenate([top, jnp.zeros((items, items), F32)], axis=1),
                jnp.concatenate([corner, bottom], axis=1),
            ],
            axis=0,
        )
        inverse_pair = split(inverse)
        need(later_dyn, second, first, own_weights, own_upper, pack, seen, own_cov)
        fac[...] = packed_factor(plan, ints_v, 0, pack)
        last = [jnp.transpose(own_columns(own_upper)), jnp.transpose(own_columns(fac))]

        @pl.when(info[2] == 0)
        def _():
            panel_dynamics(plan, info, ints, first, second, own_weights, split(own_upper[...]), dyn)
            out_dyn[0] = dyn[...]
            out_off[0] = own_columns(own_offset)[0:1, :]
            out_cov[0] = own_cov[...]
            out_fac[0, :, :items] = last[0]
            out_fac[0, :, items:rank] = last[1]
            out_fac[0, :, rank:] = jnp.zeros((panel, rank), F32)
            zeta = jnp.concatenate([own_small[0:1, :], own_small[1:2, :]], axis=1)
            zeta = jnp.broadcast_to(zeta, (SMALL, rank))
            out_info[0] = mm(zeta, out_fac[0, :, :rank], NT)[0:1, :]

        @pl.when(info[2] == 1)
        def _():
            weights[...] = dot3(split(carried[...]), inverse_pair, NT)
            own_weight = weights[mine, :]
            weight_pair = split(-own_weight)
            left = later_dyn[...] + dot3(split(dot3(weight_pair, inverse_pair, NN)), factor_pair, NN)
            left_pair = split(left)
            out_cov[0] = half[...] + dot3(weight_pair, split(weights[...]), NT)
            across(
                plan, ints, 1, lambda i, c: columns_of(left_pair, block(plan, c)),
                lambda c: second[block(plan, c), :], half,
            )
            middle = split(half[...])
            across(
                plan, ints, 0, lambda i, c: columns_of(middle, block(plan, c)),
                lambda c: first[block(plan, c), :], dyn,
            )
            through = split(dot3(left_pair, split(own_weights[...]), NN))
            out_dyn[0] = dyn[...] - dot3(through, split(own_upper[...]), NN)
            residual = jnp.concatenate([later_small[0:1, :], later_small[1:2, :]], axis=1)
            offset = own_offset[...]
            residual = jnp.broadcast_to(residual, (SMALL, rank)) - dot3(split(offset), factor_pair, NT)
            solved = dot3(split(residual), inverse_pair, NT)
            gone = mm(offset, later_dyn[...], NT) + mm(solved, own_weight, NT)
            out_off[0] = gone[0:1, :] + later_offset[0:1, :]
            out_fac[0, :, :rank] = jnp.transpose(dot3(inverse_pair, split(seen[...]), NN))
            out_fac[0, :, rank : rank + items] = last[0]
            out_fac[0, :, rank + items :] = last[1]
            zeta = jnp.concatenate([solved[0:1, :], own_small[0:1, :], own_small[1:2, :]], axis=1)
            zeta = jnp.broadcast_to(zeta, (SMALL, 2 * rank))
            out_info[0] = mm(zeta, out_fac[0], NT)[0:1, :]

    even, odd = later_gains
    first, second, own_weights, own_upper, own_small, own_offset = own
    later_first, later_second, later_weights, later_upper, later_small, later_dyn, later_offset = later
    own_cov, later_cov = covs
    return lazy_call(
        body,
        "finish",
        [
            (1, panel, states),
            (1, 1, panel),
            (1, panel, states),
            (1, panel, 2 * rank),
            (1, 1, panel),
        ],
        (info, ints, later_ints, ints, later_ints, own_small, own_offset, later_small, later_offset),
        [SM] * 3 + [VM] * 6,
        (
            even, odd, later_upper, later_pack, later_first, later_second, later_weights, moved, later_cov,
            later_dyn, second, first, own_weights, own_upper, pack, seen, own_cov,
        ),
        scratch=[pltpu.VMEM((states, rank), BF16)] * 4
        + [pltpu.VMEM((panel, states), BF16)] * 4
        + [pltpu.VMEM((states, rank), F32)] * 2
        + [pltpu.VMEM((items, states), F32)]
        + [pltpu.VMEM((panel, states), F32)] * 2,
        micros=20,
    )


def per_device(mesh, dyn_pattern, dyn_values, offsets, covariance, obs_block, obs_matrix, obs_data):
    plan = Plan(mesh, dyn_pattern, dyn_values, obs_block, obs_matrix)
    here = lax.axis_index(PLANE)
    even_turn = 1 - lax.axis_index("tm") % 2
    info = jnp.stack([here, lax.axis_index("obs"), even_turn]).astype(jnp.int32)
    ints = jnp.concatenate([obs_block, dyn_pattern.reshape(2, -1)], axis=1)

    pieces = [obs_matrix] + [exchange(obs_matrix, "obs", k, plan.obs) for k in range(1, plan.obs)]
    later_ints = earlier(plan, ints)
    own_first, own_second = dyn_values[0], dyn_values[1]
    pieces, own_first, own_second = tie(pieces, own_first, own_second)
    later_values = earlier(plan, own_first)
    message, obs = gain_step(plan, info, obs_block, pieces, covariance, offsets, obs_data)
    gain_leg_one = first_leg(plan, message)
    gain_leg_one, own_second, own_first, later_ints = tie(gain_leg_one, own_second, own_first, later_ints)
    gain_even, gain_odd = second_leg(plan, gain_leg_one)
    later_gain_even = earlier(plan, gain_even)
    second_leg_one = first_leg(plan, own_second)
    gains, pack = system_step(plan, info, ints, gain_even, gain_odd, obs)
    pack, second_leg_one, own_first, later_values, later_gain_even = tie(
        pack, second_leg_one, own_first, later_values, later_gain_even
    )
    later_pack = earlier(plan, pack)
    second_even, second_odd = second_leg(plan, second_leg_one)
    later_second_even = earlier(plan, second_even)
    first_leg_one = first_leg(plan, own_first)

    spread, second = spread_step(plan, info, ints, second_even, second_odd, covariance)
    first_leg_one, second, later_values, later_pack, later_gain_even = tie(
        first_leg_one, second, later_values, later_pack, later_gain_even
    )
    moved = swap_blocks(plan, spread.reshape(plan.n, plan.panel, plan.panel))
    first_even, first_odd = second_leg(plan, first_leg_one)
    later_leg_one = first_leg(plan, later_values)
    later_gain_odd = other_core(plan, later_gain_even, gain_odd)
    first, weights, upper, small = level_step(plan, info, ints, first_even, first_odd, second, gains, pack)
    moved, weights, later_leg_one = tie(moved, weights, later_leg_one)
    later_even, later_odd = second_leg(plan, later_leg_one)
    cov, offset = covariance_step(plan, info, ints, moved, second, weights, covariance, pack, small)
    later_second_even, offset = tie(later_second_even, offset)
    later_second_odd = other_core(plan, later_second_even, second_odd)
    own = (first, second, weights, upper, small, offset)
    later_cov = earlier(plan, cov)

    later_first, later_upper = later_upper_step(plan, info, later_ints, later_even, later_odd, later_pack)
    gain = later_gain_step(plan, later_ints, cov, later_upper, later_pack)
    gain_leg_one = first_leg(plan, gain)
    later_second, later_weights, spread = later_level_step(
        plan, info, later_ints, later_second_even, later_second_odd, later_gain_even, later_gain_odd,
        later_first, later_upper, later_pack, cov,
    )
    moved = swap_blocks(plan, spread.reshape(plan.n, plan.panel, plan.panel))
    gain_leg_one, later_weights = tie(gain_leg_one, later_weights)
    gain_even, gain_odd = second_leg(plan, gain_leg_one)
    seen, later_dyn, later_small, later_offset = ahead_step(
        plan, info, ints, later_ints, first, second, weights, upper,
        later_first, later_second, later_weights, later_upper, later_pack,
    )
    later = (later_first, later_second, later_weights, later_upper, later_small, later_dyn, later_offset)
    dyn, off, cov, fac, information = finish_step(
        plan, info, ints, later_ints, own, later, (cov, later_cov), (gain_even, gain_odd), moved, seen, pack, later_pack
    )
    return dyn, off[:, 0], cov, fac, information[:, 0]


def solution(mesh):
    placed = (
        P("tm", None, None),
        P("tm", PLANE, None),
        P("tm", PLANE),
        P("tm", PLANE, None),
        P("tm", None),
        P("tm", "obs", None),
        P("tm", "obs"),
    )

    def run(*arrays):
        return per_device(mesh, *arrays)

    return jax.shard_map(
        run,
        mesh=mesh,
        in_specs=placed,
        out_specs=(
            P("tm", PLANE, None),
            P("tm", PLANE),
            P("tm", PLANE, None),
            P("tm", PLANE, None),
            P("tm", PLANE),
        ),
        check_vma=False,
    )
```
